32 devices in a mesh: grp: 2 (over y), ao: 4 (over z), vir: 2 (over x), rep: 2 (over core).
Axes of the slice: x: 2, y: 2, z: 4, core: 2. Of those that a mesh axis runs over, the one named last changes fastest.
Arguments:
- half_ints: bfloat16 [8, 2, 24, 128, 128], P('grp', 'rep', 'ao'), parts along dimension 0, may hold values from -6 to 6
- coeff: bfloat16 [2560, 2048], P('rep', 'ao'), may hold values from -0.15625 to 0.15625
- eps_occ: float32 [400], replicated, may hold values from -1.5 to -0.5
- eps_vir: float32 [2048], replicated, may hold values from 0.5 to 2.5
- pair_occ: int32 [8, 2], P(('grp', 'ao')), parts along dimension 0, may hold values from 0 to 399
- tile_list: int32 [2, 24, 2], P('rep'), may hold values from 0 to 23, as said below
- shell_extra: int32 [2, 12], replicated, may hold values from 1 to 64, 512 in all within a row
Outputs:
- amplitudes: bfloat16 [8, 2048, 2048], P(('grp', 'ao'), 'rep', 'vir'), parts along dimension 0
The draws below stay inside these ranges and needn't reach their ends.
There are 2 independent parts, one for each index of `grp`. The reference program is written for one: setup_inputs(seed, part) draws one part's arguments, and reference() takes and returns one part's arrays. A program takes and returns all parts, laid end to end along the dimension named above; an argument that names none is the same for every part. Nothing has to cross between parts.
Inputs may be any that keep to these rules, and one draw needn't show every extreme that they name: `tile_list`: column 0 is a row block within the half, below 12; column 1 is a block of all 24; every half has the tile (11, 23). `shell_extra`: each row sums to 512.
All inputs are finite; a program needn't handle non-finite values.
Results may differ from the reference program's by a relative error of at most 0.0085.
Values may be sent and summed in bfloat16 or wider, within the bound.
No kernel may reach another device: no remote copies, remote signals or barrier semaphores. Data moves between devices by JAX's collectives and lax.ppermute only.
A program may use at most 128 MiB of HBM per device.

```python
import math
import jax
import jax.numpy as jnp
import numpy as np
from jax import lax

NAO = 2560
NV = 2048
NOCC = 400
TILE = 128
HALF_BLK = 12
NPAIR = 4
NBLK = 24
TILES_HALF = 24
N_REP = 2


def draw_tile_list(key, part):
    key = jax.random.fold_in(key, 7)
    halves = NBLK // HALF_BLK
    cells = HALF_BLK * NBLK
    keys = jax.random.split(key, halves)
    picked = jax.vmap(lambda one_key: jax.random.permutation(one_key, cells)[:TILES_HALF])(keys)
    picked = picked.at[:, 0].set(cells - 1)
    return jnp.stack([picked // NBLK, picked % NBLK], axis=-1).astype(jnp.int32)


def with_ends(result, stream_key, least, largest):
    longest = result.shape.index(max(result.shape))
    spots = []
    for shift in (0, 1):
        where = [jax.random.randint(jax.random.fold_in(stream_key, axis), (), 0, length) for axis, length in enumerate(result.shape)]
        where[longest] = (where[longest] + shift) % result.shape[longest]
        spots.append(tuple(where))
    return result.at[spots[0]].set(least).at[spots[1]].set(largest)


def shard_levels(stream_key, shape, cuts, smallest, largest):
    def one(position, parts):
        draws = jax.random.uniform(jax.random.fold_in(jax.random.fold_in(stream_key, 6), position), (parts,), jnp.float32, smallest / len(cuts), largest / len(cuts))
        return jnp.repeat(jnp.exp(draws), shape[position] // parts).reshape((-1,) + (1,) * (len(shape) - position - 1))

    loudness = one(*cuts[0])
    for cut in cuts[1:]:
        loudness = loudness * one(*cut)
    return loudness


def length_profile(amount, total, bound, slope):
    weights = [(1 << 20) // math.isqrt(rank ** slope) + 1 for rank in range(2, amount + 1)]
    surplus, holding = total - bound - (amount - 1), [1] * (amount - 1)
    while surplus > 0:
        candidates = [i for i in range(amount - 1) if holding[i] < bound]
        mass, remaining = sum([weights[i] for i in candidates]), surplus
        for i in candidates:
            more = min(bound - holding[i], max(1, remaining * weights[i] // mass), surplus)
            holding[i] = holding[i] + more
            surplus = surplus - more
    return np.array([bound] + holding)


def uneven(rng, amount, total, reach, skew):
    if amount == 2:
        one = jax.random.randint(rng, (), max(1, total - reach), min(reach, total - 1) + 1)
        return jnp.stack([one, total - one])
    lengths = jnp.asarray(length_profile(amount, total, reach, skew), jnp.int32)
    twos = (amount - 1) // 2
    giver, sink = lengths[1:1 + 2 * twos:2], lengths[2:2 + 2 * twos:2]
    room = jnp.minimum(giver - 1, reach - sink)
    passed = jax.random.randint(jax.random.fold_in(rng, 1), (twos,), 0, 1 << 20) % (room + 1)
    lengths = lengths.at[1:1 + 2 * twos:2].set(giver - passed).at[2:2 + 2 * twos:2].set(sink + passed)
    return lengths[jax.random.permutation(jax.random.fold_in(rng, 2), amount)]


def bell_draw(own_key, shape, deviation, limit, cuts=(), kind=jnp.bfloat16):
    loudness = shard_levels(own_key, shape, cuts, -0.22, 0.18) if cuts else 1.0
    entries = jax.random.normal(own_key, shape, jnp.float32) * deviation * loudness
    return jnp.minimum(jnp.maximum(entries, -limit), limit).astype(kind)


def setup_inputs(seed: int = 0, part: int = 0) -> dict:
    key_list = jax.random.split(jax.random.key(seed), 8)
    part_keys = jax.random.split(jax.random.fold_in(key_list[7], part), 8)
    return {
        "half_ints": bell_draw(part_keys[0], (NPAIR, N_REP, TILES_HALF, TILE, TILE), 1.0, 6.0, ((1, 2), (2, 4))),
        "coeff": bell_draw(key_list[1], (NAO, NV), (NAO // 2) ** -0.5, 0.15625, ((0, 2), (1, 4))),
        "eps_occ": jnp.clip(jax.random.uniform(key_list[2], (NOCC,), jnp.float32, -1.5, -0.5), -1.5, -0.5),
        "eps_vir": jnp.clip(jax.random.uniform(key_list[3], (NV,), jnp.float32, 0.5, 2.5), 0.5, 2.5),
        "pair_occ": with_ends(jax.random.randint(part_keys[4], (NPAIR, 2), 0, NOCC), jax.random.fold_in(part_keys[4], 1), 0, NOCC - 1).astype(jnp.int32),
        "tile_list": draw_tile_list(jax.random.fold_in(key_list[7], 71), part),
        "shell_extra": jax.vmap(lambda own: uneven(own, HALF_BLK, NAO // N_REP - (TILE // 2) * HALF_BLK, TILE // 2, 0))(jax.random.split(key_list[6], N_REP)).reshape((N_REP, HALF_BLK)).astype(jnp.int32),
    }


def block_layout(shell_extra):
    shell_sizes = (TILE // 2 + shell_extra).reshape(-1).astype(jnp.int32)
    offsets = (jnp.cumsum(shell_sizes) - shell_sizes).astype(jnp.int32)
    columns = jnp.arange(TILE, dtype=jnp.int32)
    real_rows = offsets[:, None] + columns[None, :]
    valid_rows = columns[None, :] < shell_sizes[:, None]
    return offsets, real_rows, valid_rows


def padded_rows(matrix, real_rows, valid_rows):
    picked = jnp.take(matrix, jnp.minimum(real_rows, NAO - 1).reshape(-1), axis=0)
    picked = picked.reshape(real_rows.shape[0], TILE, matrix.shape[1])
    return jnp.where(valid_rows[:, :, None], picked, jnp.zeros_like(picked))


def packed_position(partial_starts, partial_length):
    positions = jnp.arange(partial_length, dtype=jnp.int32)
    block_of = jnp.sum((partial_starts[None, :] <= positions[:, None]).astype(jnp.int32), axis=1) - 1
    block_start = jnp.take(partial_starts, block_of)
    return (block_of * TILE + positions - block_start).astype(jnp.int32)


def reference(half_ints, coeff, eps_occ, eps_vir, pair_occ, tile_list, shell_extra):
    offsets, real_rows, valid_rows = block_layout(shell_extra)
    coeff_pad = padded_rows(coeff, real_rows, valid_rows)
    partial_length = NAO // N_REP
    packed_tiles = []
    for partial_integrals in range(N_REP):
        partial_starts = offsets[partial_integrals * HALF_BLK:(partial_integrals + 1) * HALF_BLK] - partial_integrals * partial_length
        packed_tiles.append(packed_position(partial_starts, partial_length))
    blocks = jnp.arange(HALF_BLK, dtype=jnp.int32)

    def one_pair(index):
        tiles_all, pair = index
        total = jnp.zeros((NV, NV), jnp.float32)
        for partial_integrals in range(N_REP):
            coeff_nu = jnp.take(coeff_pad, tile_list[partial_integrals, :, 1], axis=0).astype(jnp.float32)
            products = jnp.einsum('tij,tjb->tib', tiles_all[partial_integrals].astype(jnp.float32), coeff_nu)
            one_hot = (tile_list[partial_integrals, :, 0][:, None] == blocks[None, :]).astype(jnp.float32)
            padded_partial = jnp.einsum('tm,tib->mib', one_hot, products, precision=lax.Precision.HIGHEST)
            padded_partial = padded_partial.astype(jnp.bfloat16).reshape(HALF_BLK * TILE, NV)
            packed_tile = jnp.take(padded_partial, packed_tiles[partial_integrals], axis=0)
            coeff_half = coeff[partial_integrals * partial_length:(partial_integrals + 1) * partial_length]
            partial_sum = jnp.dot(coeff_half.T, packed_tile, preferred_element_type=jnp.float32)
            rounded = lax.optimization_barrier(partial_sum.astype(jnp.bfloat16))
            total = total + rounded.astype(jnp.float32)
        pair_energy = jnp.take(eps_occ, pair[0]) + jnp.take(eps_occ, pair[1])
        denominator = pair_energy - eps_vir[:, None] - eps_vir[None, :]
        return (total / denominator).astype(jnp.bfloat16)

    return lax.map(one_pair, (half_ints, pair_occ))
```

```python
import functools

import jax
import jax.numpy as jnp
from jax import lax
from jax.experimental import pallas as pl
from jax.experimental.pallas import tpu as pltpu
from jax.sharding import PartitionSpec as P

TILE = 128
HALF_BLK = 12
LANES = 128
ROWS_WIN = 144
COLS_WIN = 256
RING = (0, 1, 3, 2)
SWAP = ((0, 1), (1, 0))
F32 = jnp.float32
BF16 = jnp.bfloat16


def shift_kernel(per_slot, n_refs, n_ao, row_total, *refs):
    place, list_own, list_other, extra = refs[:4]
    tiles = refs[4 : 4 + n_refs]
    shifted, row_base, col_base, offsets = refs[4 + n_refs :]
    blocks = 2 * HALF_BLK

    def lay(k, start):
        offsets[k] = start
        return start + TILE // 2 + extra[k // HALF_BLK, lax.rem(k, HALF_BLK)]

    lax.fori_loop(0, blocks, lay, jnp.int32(0))
    rows = lax.broadcasted_iota(jnp.int32, (TILE, TILE), 0)
    cols = lax.broadcasted_iota(jnp.int32, (TILE, TILE), 1)
    for r in range(n_refs):
        other, slot = r // (n_refs // 2), r % (n_refs // 2)
        listed = list_other if other else list_own
        half = place[0] if not other else 1 - place[0]
        ref = tiles[r]
        count = ref.shape[0]

        def one(i, carry, ref=ref, listed=listed, half=half, slot=slot, r=r, count=count):
            n = place[1 + slot] * count + i
            m = listed[0, n, 0] + HALF_BLK * half
            k = listed[0, n, 1]
            size_m = TILE // 2 + extra[m // HALF_BLK, lax.rem(m, HALF_BLK)]
            size_k = TILE // 2 + extra[k // HALF_BLK, lax.rem(k, HALF_BLK)]
            off_m = offsets[m]
            off_k = offsets[k]
            base_m = (off_m // 16) * 16
            base_k = jnp.minimum((off_k // LANES) * LANES, row_total - COLS_WIN)
            value = jnp.where((rows < size_m) & (cols < size_k), ref[i].astype(F32), 0.0)
            value = jnp.concatenate([value, jnp.zeros((TILE, COLS_WIN - TILE), F32)], axis=1)
            value = jnp.concatenate(
                [value, jnp.zeros((ROWS_WIN - TILE, COLS_WIN), F32)], axis=0
            )
            value = pltpu.roll(value, off_k - base_k, 1)
            value = pltpu.roll(value, off_m - base_m, 0)
            at = r * count + i
            shifted[at] = value.astype(BF16)
            row_base[at] = base_m
            col_base[at] = base_k
            return carry

        lax.fori_loop(0, count, one, 0)


def shift_tiles(place, list_own, list_other, shell_extra, tiles, row_total):
    count = tiles[0].shape[0]
    total = len(tiles) * count
    smem = pl.BlockSpec(memory_space=pltpu.SMEM)
    vmem = pl.BlockSpec(memory_space=pltpu.VMEM)
    return pl.pallas_call(
        functools.partial(shift_kernel, count, len(tiles), len(tiles) // 2, row_total),
        out_shape=(
            jax.ShapeDtypeStruct((total, ROWS_WIN, COLS_WIN), BF16),
            jax.ShapeDtypeStruct((total,), jnp.int32),
            jax.ShapeDtypeStruct((total,), jnp.int32),
        ),
        in_specs=[smem] * 4 + [vmem] * len(tiles),
        out_specs=(vmem, smem, smem),
        scratch_shapes=[pltpu.SMEM((2 * HALF_BLK,), jnp.int32)],
        compiler_params=pltpu.CompilerParams(vmem_limit_bytes=32 << 20),
        name="shift_tiles",
    )(place, list_own, list_other, shell_extra, *tiles)


def transform_kernel(layout, n_tiles, a_panels, b_panels, step_panels, *refs):
    place, row_base, col_base, pair_occ, eps_occ = refs[:5]
    shifted, eps_rows, eps_cols = refs[5:8]
    pieces = refs[8 : 8 + len(layout)]
    out, panels, total, held, sems = refs[8 + len(layout) :]
    step = pl.program_id(0)
    width = b_panels * LANES
    b_first = place[1] * b_panels
    row_total = panels.shape[1]

    @pl.when(step == 0)
    def _():
        copies = []
        for ref, (at, column, half_at, row) in zip(pieces, layout):
            rows = ref.shape[0]
            start = pl.multiple_of(place[half_at] * (row_total // 2) + row, 16)
            copies.append(
                pltpu.make_async_copy(
                    ref.at[:, pl.ds(column * LANES, LANES)],
                    panels.at[place[at], pl.ds(start, rows), :],
                    sems.at[len(copies)],
                )
            )
        for copy in copies:
            copy.start()
        total[...] = jnp.zeros_like(total)
        for copy in copies:
            copy.wait()

        def add(n, carry):
            base_m = pl.multiple_of(row_base[n], 16)
            base_k = pl.multiple_of(col_base[n], LANES)
            window = jnp.concatenate(
                [panels[b_first + j, pl.ds(base_k, COLS_WIN), :] for j in range(b_panels)], axis=1
            )
            total[pl.ds(base_m, ROWS_WIN), :] += jnp.dot(
                shifted[n], window, preferred_element_type=F32
            )
            return carry

        lax.fori_loop(0, n_tiles, add, 0)
        held[...] = total[pl.ds(0, row_total), :].astype(BF16)

    a_first = place[0] * a_panels + step * step_panels
    left = jnp.concatenate([panels[a_first + j] for j in range(step_panels)], axis=1)
    product = lax.dot_general(
        left, held[...], (((0,), (0,)), ((), ())), preferred_element_type=F32
    )
    energy = eps_occ[pair_occ[0, 0]] + eps_occ[pair_occ[0, 1]]
    denominator = energy - eps_rows[...] - eps_cols[pl.ds(place[1], 1), :]
    out[0] = (product / denominator).astype(BF16)


def transform(place, layout, bases, pair_occ, eps_occ, shifted, eps_vir, pieces, sizes):
    row_total, a_width, b_width, full_width = sizes
    a_panels, b_panels = a_width // LANES, b_width // LANES
    step_panels = 2
    steps = a_panels // step_panels
    n_tiles = shifted.shape[0]
    row_base, col_base = bases
    smem = pl.BlockSpec(memory_space=pltpu.SMEM)
    vmem = pl.BlockSpec(memory_space=pltpu.VMEM)
    refs = [pieces[piece[0]] for piece in layout]
    own_rows = lax.dynamic_slice_in_dim(eps_vir, lax.axis_index("rep") * a_width, a_width, 0)
    return pl.pallas_call(
        functools.partial(
            transform_kernel, [piece[1:] for piece in layout], n_tiles, a_panels, b_panels,
            step_panels,
        ),
        grid=(steps,),
        out_shape=jax.ShapeDtypeStruct((1, a_width, b_width), BF16),
        in_specs=[smem] * 5
        + [vmem, pl.BlockSpec((step_panels * LANES, 1), lambda i: (i, 0)), vmem]
        + [pl.BlockSpec(memory_space=pl.ANY)] * len(refs),
        out_specs=pl.BlockSpec((1, step_panels * LANES, b_width), lambda i: (0, i, 0)),
        scratch_shapes=[
            pltpu.VMEM((full_width // LANES, row_total, LANES), BF16),
            pltpu.VMEM((row_total + TILE, b_width), F32),
            pltpu.VMEM((row_total, b_width), BF16),
            pltpu.SemaphoreType.DMA((len(refs),)),
        ],
        compiler_params=pltpu.CompilerParams(vmem_limit_bytes=48 << 20),
        name="transform",
    )(
        place, row_base, col_base, pair_occ, eps_occ,
        shifted, own_rows.reshape(a_width, 1), eps_vir.reshape(-1, b_width), *refs,
    )


def ring_pairs(distance):
    return [(RING[i], RING[(i + distance) % 4]) for i in range(4)]


def other_core(value):
    return lax.ppermute(value, "rep", SWAP)


def exchange_small(half_ints, coeff):
    z, x, y = lax.axis_index("ao"), lax.axis_index("vir"), lax.axis_index("grp")
    ring = jnp.asarray(RING, jnp.int32)
    spot = jnp.where(z == 3, 2, jnp.where(z == 2, 3, z))
    quarter = y * 2 + x
    shards = [ring[(spot - k) % 4] for k in range(4)]
    rows, width = coeff.shape
    part = width // LANES
    middle = rows // 2
    moving = lax.dynamic_slice_in_dim(coeff, quarter * LANES, LANES, 1)
    pieces = [(coeff, 4 * shards[0] + j, j, 0) for j in range(part)]
    tiles = [lax.dynamic_index_in_dim(half_ints[:, 0], z, 0, False)]
    for k in (1, 2, 3):
        moving = lax.ppermute(moving, "ao", ring_pairs(1))
        leaving = lax.dynamic_index_in_dim(half_ints[:, 0], ring[(spot + k) % 4], 0, False)
        tiles.append(lax.ppermute(leaving, "ao", ring_pairs(k)))
        by_x = lax.ppermute(moving, "vir", SWAP)
        by_y = lax.ppermute(moving, "grp", SWAP)
        far_x = lax.ppermute(by_y[:middle], "vir", SWAP)
        far_y = lax.ppermute(by_x[middle:], "grp", SWAP)
        first = part * shards[k]
        pieces += [
            (moving, first + quarter, 0, 0),
            (by_x, first + (quarter ^ 1), 0, 0),
            (by_y, first + (quarter ^ 2), 0, 0),
            (far_x, first + (quarter ^ 3), 0, 0),
            (far_y, first + (quarter ^ 3), 0, middle),
        ]
    return pieces, tiles, shards


def exchange_any(half_ints, coeff):
    count = lax.axis_size("ao")
    part = coeff.shape[1] // LANES
    gathered = lax.all_gather(coeff, "ao", axis=0, tiled=False)
    tiles = lax.all_to_all(half_ints, "ao", split_axis=0, concat_axis=2, tiled=True)[0, 0]
    tiles = tiles.reshape((count, -1) + tiles.shape[1:])
    pieces = [
        (gathered[s], jnp.int32(s * part + j), j, 0) for s in range(count) for j in range(part)
    ]
    return pieces, [tiles[s] for s in range(count)], [jnp.int32(s) for s in range(count)]


def local(half_ints, coeff, eps_occ, eps_vir, pair_occ, tile_list, shell_extra):
    sizes = tuple(lax.axis_size(name) for name in ("grp", "ao", "vir"))
    rows, width = coeff.shape
    row_total = rows * lax.axis_size("rep")
    full_width = width * sizes[1]
    small = sizes == (2, 4, 2) and width == 4 * LANES
    pieces, tiles, order = (exchange_small if small else exchange_any)(half_ints, coeff)
    core = lax.axis_index("rep").astype(jnp.int32)
    vir = lax.axis_index("vir").astype(jnp.int32)

    swapped = {}
    arrays, layout, ids = [], [], []
    for piece, panel, column, row in pieces:
        if id(piece) not in swapped:
            swapped[id(piece)] = len(arrays)
            arrays += [piece, other_core(piece)]
        at = swapped[id(piece)]
        ids.append(panel)
        layout.append((at, 3 + len(ids), column, 2, row))
        layout.append((at + 1, 3 + len(ids), column, 3, row))
    place = jnp.stack([core, vir, core, 1 - core] + [jnp.asarray(i, jnp.int32) for i in ids])

    tile_place = jnp.stack([core] + [jnp.asarray(s, jnp.int32) for s in order])
    all_tiles = tiles + [other_core(t) for t in tiles]
    shifted, row_base, col_base = shift_tiles(
        tile_place, tile_list, other_core(tile_list), shell_extra, all_tiles, row_total
    )
    return transform(
        place, layout, (row_base, col_base), pair_occ, eps_occ, shifted, eps_vir, arrays,
        (row_total, full_width // lax.axis_size("rep"), full_width // sizes[2], full_width),
    )


def solution(mesh):
    in_specs = (
        P("grp", "rep", "ao", None, None),
        P("rep", "ao"),
        P(),
        P(),
        P(("grp", "ao"), None),
        P("rep", None, None),
        P(),
    )
    out_specs = P(("grp", "ao"), "rep", "vir")
    return jax.shard_map(local, mesh=mesh, in_specs=in_specs, out_specs=out_specs, check_vma=False)
```

```python
import functools

import jax
import jax.numpy as jnp
from jax import lax
from jax.experimental import pallas as pl
from jax.experimental.pallas import tpu as pltpu
from jax.sharding import PartitionSpec as P

TILE = 128
HALF_BLK = 12
LANES = 128
ROWS_WIN = 144
COLS_WIN = 256
GROUPS = 4
RING = (0, 1, 3, 2)
SWAP = ((0, 1), (1, 0))
F32 = jnp.float32
BF16 = jnp.bfloat16
SMEM = pl.BlockSpec(memory_space=pltpu.SMEM)
VMEM = pl.BlockSpec(memory_space=pltpu.VMEM)
MIB = 1 << 20


def shift_kernel(rows_half, n_refs, *refs):
    place, listed, extra = refs[:3]
    tiles = refs[3 : 3 + n_refs]
    shifted, where, offsets = refs[3 + n_refs :]

    def lay(k, start):
        start = jnp.where(k == HALF_BLK, 0, start)
        offsets[k] = start
        return start + TILE // 2 + extra[k // HALF_BLK, lax.rem(k, HALF_BLK)]

    lax.fori_loop(0, 2 * HALF_BLK, lay, jnp.int32(0))
    rows = lax.broadcasted_iota(jnp.int32, (TILE, TILE), 0)
    cols = lax.broadcasted_iota(jnp.int32, (TILE, TILE), 1)
    for r in range(n_refs):
        ref = tiles[r]
        count = ref.shape[0]

        def one(i, carry, ref=ref, r=r, count=count):
            n = place[1 + r] * count + i
            m = listed[0, n, 0]
            k = listed[0, n, 1]
            half_k = k // HALF_BLK
            size_m = TILE // 2 + extra[place[0], m]
            size_k = TILE // 2 + extra[half_k, lax.rem(k, HALF_BLK)]
            off_m = offsets[place[0] * HALF_BLK + m]
            off_k = offsets[k]
            base_m = (off_m // 16) * 16
            base_k = jnp.minimum((off_k // LANES) * LANES, rows_half - COLS_WIN)
            value = jnp.where((rows < size_m) & (cols < size_k), ref[i].astype(F32), 0.0)
            value = jnp.concatenate([value, jnp.zeros((TILE, COLS_WIN - TILE), F32)], axis=1)
            value = jnp.concatenate(
                [value, jnp.zeros((ROWS_WIN - TILE, COLS_WIN), F32)], axis=0
            )
            value = pltpu.roll(value, off_k - base_k, 1)
            value = pltpu.roll(value, off_m - base_m, 0)
            at = r * count + i
            shifted[at] = value.astype(BF16)
            where[0, at] = base_m
            where[1, at] = base_k
            where[2, at] = jnp.where(half_k == place[0], 0, 1)
            return carry

        lax.fori_loop(0, count, one, 0)


def shift_tiles(place, listed, shell_extra, tiles, rows_half):
    total = sum(t.shape[0] for t in tiles)
    return pl.pallas_call(
        functools.partial(shift_kernel, rows_half, len(tiles)),
        out_shape=(
            jax.ShapeDtypeStruct((total, ROWS_WIN, COLS_WIN), BF16),
            jax.ShapeDtypeStruct((3, total), jnp.int32),
        ),
        in_specs=[SMEM] * 3 + [VMEM] * len(tiles),
        out_specs=(VMEM, SMEM),
        scratch_shapes=[pltpu.SMEM((2 * HALF_BLK,), jnp.int32)],
        compiler_params=pltpu.CompilerParams(vmem_limit_bytes=12 * MIB),
        cost_estimate=pl.CostEstimate(flops=0, bytes_accessed=8 * MIB, transcendentals=0),
        name="shift_tiles",
    )(place, listed, shell_extra, *tiles)


def assemble_kernel(quarter, own, by_x, by_y, far_x, far_y, out):
    rows = own.shape[0]

    def put(at, value, first):
        start = pl.multiple_of(at * LANES, LANES)
        out[first : first + value.shape[0], pl.ds(start, LANES)] = value

    q = quarter[0]
    put(q, own[...], 0)
    put(q ^ 1, by_x[:rows], 0)
    put(q ^ 2, by_y[:rows], 0)
    half = rows // 2
    put(q ^ 3, far_x[far_x.shape[0] - half :], 0)
    put(q ^ 3, far_y[far_y.shape[0] - half :], half)


def assemble(quarter, *pieces):
    rows = pieces[0].shape[0]
    return pl.pallas_call(
        assemble_kernel,
        out_shape=jax.ShapeDtypeStruct((rows, 4 * LANES), BF16),
        in_specs=[SMEM] + [VMEM] * 5,
        out_specs=VMEM,
        compiler_params=pltpu.CompilerParams(vmem_limit_bytes=8 * MIB),
        cost_estimate=pl.CostEstimate(flops=0, bytes_accessed=3 * MIB, transcendentals=0),
        name="assemble",
    )(quarter, *pieces)


def first_kernel(n_refs, n_tiles, ids, where, shifted, *refs):
    own = refs[:n_refs]
    other = refs[n_refs : 2 * n_refs]
    out, held, total = refs[2 * n_refs :]
    blocks = held.shape[1]
    for s in range(n_refs):
        at = ids[s]

        @pl.when((at >= 0) & (at < blocks))
        def _(s=s, at=at):
            held[0, at] = own[s][...]
            held[1, at] = other[s][...]

    total[...] = jnp.zeros_like(total)

    def add(n, carry):
        base_m = pl.multiple_of(where[0, n], 16)
        base_k = pl.multiple_of(where[1, n], LANES)
        half = where[2, n]
        for j in range(blocks):
            total[j, pl.ds(base_m, ROWS_WIN), :] += jnp.dot(
                shifted[n], held[half, j, pl.ds(base_k, COLS_WIN), :],
                preferred_element_type=F32,
            )
        return carry

    lax.fori_loop(0, n_tiles, add, 0)
    out[...] = total[:, : out.shape[1], :].astype(BF16)


def first_product(ids, where, shifted, own, other, blocks):
    rows, width = own[0].shape
    n_tiles = shifted.shape[0]
    return pl.pallas_call(
        functools.partial(first_kernel, len(own), n_tiles),
        out_shape=jax.ShapeDtypeStruct((blocks, rows, width), BF16),
        in_specs=[SMEM] * 2 + [VMEM] * (1 + 2 * len(own)),
        out_specs=VMEM,
        scratch_shapes=[
            pltpu.VMEM((2, blocks, rows, width), BF16),
            pltpu.VMEM((blocks, rows + TILE, width), F32),
        ],
        compiler_params=pltpu.CompilerParams(vmem_limit_bytes=20 * MIB),
        cost_estimate=pl.CostEstimate(
            flops=n_tiles * 2 * ROWS_WIN * COLS_WIN * width * blocks, bytes_accessed=20 * MIB,
            transcendentals=0,
        ),
        name="first_product",
    )(ids, where, shifted, *own, *other)


def pick(ids, wanted, refs, held):
    for s, ref in enumerate(refs):

        @pl.when(ids[s] == wanted)
        def _(ref=ref):
            held[...] = ref[...]


def second(held, middle):
    dims = (((0,), (0,)), ((), ()))
    return jnp.concatenate(
        [
            lax.dot_general(held[...], middle[j], dims, preferred_element_type=F32)
            for j in range(middle.shape[0])
        ],
        axis=1,
    )


def send_kernel(chunk, ids, place, middle, *refs):
    groups = refs[:GROUPS]
    out, held = refs[GROUPS:]
    pick(ids, (1 - place[0]) * (GROUPS // 2) + chunk, groups, held)
    out[...] = second(held, middle).astype(BF16)


def keep_kernel(chunk, ids, place, pair_occ, eps_occ, middle, eps_rows, eps_cols, got, *refs):
    groups = refs[:GROUPS]
    out, held = refs[-2:]
    pick(ids, place[0] * (GROUPS // 2) + chunk, groups, held)
    total = second(held, middle) + got[...].astype(F32)
    energy = eps_occ[pair_occ[0, 0]] + eps_occ[pair_occ[0, 1]]
    out[0] = (total / (energy - eps_rows[...] - eps_cols[...])).astype(BF16)


def second_cost(rows, width, columns):
    return pl.CostEstimate(
        flops=2 * rows * width * columns, bytes_accessed=8 * MIB, transcendentals=0
    )


def send_product(chunk, ids, place, middle, groups):
    rows, width = groups[0].shape
    columns = middle.shape[0] * middle.shape[2]
    return pl.pallas_call(
        functools.partial(send_kernel, chunk),
        out_shape=jax.ShapeDtypeStruct((width, columns), BF16),
        in_specs=[SMEM] * 2 + [VMEM] * (1 + GROUPS),
        out_specs=VMEM,
        scratch_shapes=[pltpu.VMEM((rows, width), BF16)],
        compiler_params=pltpu.CompilerParams(vmem_limit_bytes=16 * MIB),
        cost_estimate=second_cost(rows, width, columns),
        name="send_product",
    )(ids, place, middle, *groups)


def keep_product(chunk, ids, place, pair_occ, eps_occ, middle, eps_rows, eps_cols, got, groups, before):
    rows, width = groups[0].shape
    columns = middle.shape[0] * middle.shape[2]
    extra = [] if before is None else [before]
    fixed = [ids, place, pair_occ, eps_occ, middle, eps_rows, eps_cols, got, *groups]
    whole = lambda a: pl.BlockSpec(a.shape, lambda i, n=a.ndim: (0,) * n)
    return pl.pallas_call(
        functools.partial(keep_kernel, chunk),
        grid=(1,),
        out_shape=jax.ShapeDtypeStruct((1, GROUPS // 2 * width, columns), BF16),
        in_specs=[SMEM] * 4
        + [VMEM, pl.BlockSpec((width, 1), lambda i: (chunk, 0)), VMEM, VMEM]
        + [VMEM] * GROUPS
        + [pl.BlockSpec(memory_space=pl.ANY)] * len(extra),
        out_specs=pl.BlockSpec((1, width, columns), lambda i: (0, chunk, 0)),
        scratch_shapes=[pltpu.VMEM((rows, width), BF16)],
        input_output_aliases={len(fixed): 0} if extra else {},
        compiler_params=pltpu.CompilerParams(vmem_limit_bytes=20 * MIB),
        cost_estimate=second_cost(rows, width, columns),
        name="keep_product",
    )(*fixed, *extra)


def ring_pairs(distance):
    return [(RING[i], RING[(i + distance) % 4]) for i in range(4)]


def other_core(value):
    return lax.ppermute(value, "rep", SWAP)


def to_x(value):
    return lax.ppermute(value, "vir", SWAP)


def to_y(value):
    return lax.ppermute(value, "grp", SWAP)


def to_z(value, distance=1):
    return lax.ppermute(value, "ao", ring_pairs(distance))


def exchange_small(half_ints, coeff):
    z, x, y = lax.axis_index("ao"), lax.axis_index("vir"), lax.axis_index("grp")
    ring = jnp.asarray(RING, jnp.int32)
    spot = jnp.where(z == 3, 2, jnp.where(z == 2, 3, z))
    quarter = y * 2 + x
    order = [ring[(spot - k) % 4] for k in range(4)]
    rows = coeff.shape[0]
    half = rows // 2
    together = lax.optimization_barrier
    join = lambda a, b: jnp.concatenate([a, b], axis=0)

    own = lax.dynamic_slice_in_dim(coeff, quarter * LANES, LANES, 1)
    t = [
        lax.dynamic_index_in_dim(half_ints[:, 0], ring[(spot + k) % 4], 0, False)
        for k in range(4)
    ]
    z1, t = together((to_z(own), t))
    x1, y1, z2, t = together((to_x(z1), to_y(z1), to_z(z1), t))
    x2, y2, z3, t1, t = together(
        (to_x(join(z2, y1[:half])), to_y(join(z2, x1[half:])), to_z(z2), to_z(t[1], 1), t)
    )
    x3, y3, t2, t3 = together(
        (
            to_x(join(z3, y2[:half])), to_y(join(z3, x2[half:rows])),
            to_z(t[2], 2), to_z(t[3], 3),
        )
    )
    x4, y4 = to_x(y3[:half]), to_y(x3[half:rows])
    q = quarter.astype(jnp.int32).reshape(1)
    groups = [
        coeff,
        assemble(q, z1, x1, y1, x2, y2),
        assemble(q, z2, x2, y2, x3, y3),
        assemble(q, z3, x3, y3, x4, y4),
    ]
    return groups, [t[0], t1, t2, t3], order


def exchange_any(half_ints, coeff):
    count = lax.axis_size("ao")
    gathered = lax.all_gather(coeff, "ao", axis=1, tiled=True)
    width = gathered.shape[1] // GROUPS
    tiles = lax.all_to_all(half_ints, "ao", split_axis=0, concat_axis=2, tiled=True)[0, 0]
    groups = [gathered[:, g * width : (g + 1) * width] for g in range(GROUPS)]
    return gathered, groups, [tiles], count


def local(half_ints, coeff, eps_occ, eps_vir, pair_occ, tile_list, shell_extra):
    sizes = tuple(lax.axis_size(name) for name in ("grp", "ao", "vir"))
    rows, width = coeff.shape
    full_width = width * sizes[1]
    a_width, b_width = full_width // lax.axis_size("rep"), full_width // sizes[2]
    core = lax.axis_index("rep").astype(jnp.int32)
    vir = lax.axis_index("vir").astype(jnp.int32)
    ints = lambda values: jnp.stack([jnp.asarray(v, jnp.int32) for v in values])
    if sizes == (2, 4, 2) and width == 4 * LANES:
        groups, tiles, order = exchange_small(half_ints, coeff)
        ids = ints(order)
        blocks = b_width // width
        b_ids = ids - vir * blocks
        own, tile_order = groups, order
    else:
        gathered, groups, tiles, _ = exchange_any(half_ints, coeff)
        ids = ints(range(GROUPS))
        blocks, b_ids = 1, ints([0])
        own = [lax.dynamic_slice_in_dim(gathered, vir * b_width, b_width, 1)]
        tile_order = [0]
    other = [other_core(g) for g in own]
    place = ints([core])
    shifted, where = shift_tiles(ints([core] + tile_order), tile_list, shell_extra, tiles, rows)
    middle = first_product(b_ids, where, shifted, own, other, blocks)
    rows_energy = lax.dynamic_slice_in_dim(eps_vir, core * a_width, a_width, 0).reshape(-1, 1)
    cols_energy = lax.dynamic_slice_in_dim(eps_vir, vir * b_width, b_width, 0).reshape(1, -1)
    got = [
        other_core(send_product(chunk, ids, place, middle, groups)) for chunk in range(GROUPS // 2)
    ]
    out = None
    for chunk in range(GROUPS // 2):
        out = keep_product(
            chunk, ids, place, pair_occ, eps_occ, middle, rows_energy, cols_energy, got[chunk],
            groups, out,
        )
    return out


def solution(mesh):
    in_specs = (
        P("grp", "rep", "ao", None, None),
        P("rep", "ao"),
        P(),
        P(),
        P(("grp", "ao"), None),
        P("rep", None, None),
        P(),
    )
    out_specs = P(("grp", "ao"), "rep", "vir")
    return jax.shard_map(local, mesh=mesh, in_specs=in_specs, out_specs=out_specs, check_vma=False)
```

```python
import functools

import jax
import jax.numpy as jnp
from jax import lax
from jax.experimental import pallas as pl
from jax.experimental.pallas import tpu as pltpu
from jax.sharding import PartitionSpec as P

TILE = 128
HALF_BLK = 12
LANES = 128
ROWS_WIN = 144
COLS_WIN = 256
GROUPS = 4
UNROLL = 4
RING = (0, 1, 3, 2)
SWAP = ((0, 1), (1, 0))
F32 = jnp.float32
BF16 = jnp.bfloat16
SMEM = pl.BlockSpec(memory_space=pltpu.SMEM)
VMEM = pl.BlockSpec(memory_space=pltpu.VMEM)
ANY = pl.BlockSpec(memory_space=pl.ANY)
MIB = 1 << 20


def ring_group(step):
    z = lax.axis_index("ao")
    spot = ((z ^ (z >> 1)) - step) & 3
    return spot ^ (spot >> 1)


def shift_kernel(rows_half, slots, *refs):
    listed, extra = refs[:2]
    tiles = refs[2 : 2 + len(slots)]
    shifted, where, offsets = refs[2 + len(slots) :]
    core = lax.axis_index("rep")

    def lay(k, start):
        start = jnp.where(k == HALF_BLK, 0, start)
        offsets[k] = start
        return start + TILE // 2 + extra[k // HALF_BLK, lax.rem(k, HALF_BLK)]

    lax.fori_loop(0, 2 * HALF_BLK, lay, jnp.int32(0))
    rows = lax.broadcasted_iota(jnp.int32, (TILE, TILE), 0)
    cols = lax.broadcasted_iota(jnp.int32, (TILE, TILE), 1)
    for r, slot in enumerate(slots):
        ref = tiles[r]
        count = ref.shape[0]
        first = 0 if slot is None else ring_group(slot) * count

        def one(i, carry, ref=ref, r=r, count=count, first=first):
            n = first + i
            m = listed[0, n, 0]
            k = listed[0, n, 1]
            half_k = k // HALF_BLK
            size_m = TILE // 2 + extra[core, m]
            size_k = TILE // 2 + extra[half_k, lax.rem(k, HALF_BLK)]
            off_m = offsets[core * HALF_BLK + m]
            off_k = offsets[k]
            base_m = (off_m // 16) * 16
            base_k = jnp.minimum((off_k // LANES) * LANES, rows_half - COLS_WIN)
            value = jnp.where((rows < size_m) & (cols < size_k), ref[i].astype(F32), 0.0)
            value = jnp.concatenate([value, jnp.zeros((TILE, COLS_WIN - TILE), F32)], axis=1)
            value = jnp.concatenate(
                [value, jnp.zeros((ROWS_WIN - TILE, COLS_WIN), F32)], axis=0
            )
            value = pltpu.roll(value, off_k - base_k, 1)
            value = pltpu.roll(value, off_m - base_m, 0)
            at = r * count + i
            shifted[at] = value.astype(BF16)
            where[0, at] = base_m
            where[1, at] = base_k
            where[2, at] = jnp.where(half_k == core, 0, 1)
            return carry

        lax.fori_loop(0, count, one, 0)


def shift_tiles(slots, listed, shell_extra, tiles, rows_half):
    total = sum(t.shape[0] for t in tiles)
    return pl.pallas_call(
        functools.partial(shift_kernel, rows_half, slots),
        out_shape=(
            jax.ShapeDtypeStruct((total, ROWS_WIN, COLS_WIN), BF16),
            jax.ShapeDtypeStruct((3, total), jnp.int32),
        ),
        in_specs=[SMEM] * 2 + [VMEM] * len(tiles),
        out_specs=(VMEM, SMEM),
        scratch_shapes=[pltpu.SMEM((2 * HALF_BLK,), jnp.int32)],
        compiler_params=pltpu.CompilerParams(vmem_limit_bytes=12 * MIB),
        cost_estimate=pl.CostEstimate(flops=0, bytes_accessed=8 * MIB, transcendentals=0),
        name="shift_tiles",
    )(listed, shell_extra, *tiles)


def assemble_kernel(own, by_x, by_y, far_x, far_y, out):
    rows = own.shape[0]

    def put(at, value, first):
        start = pl.multiple_of(at * LANES, LANES)
        out[first : first + value.shape[0], pl.ds(start, LANES)] = value

    q = lax.axis_index("grp") * 2 + lax.axis_index("vir")
    put(q, own[...], 0)
    put(q ^ 1, by_x[:rows], 0)
    put(q ^ 2, by_y[:rows], 0)
    half = rows // 2
    put(q ^ 3, far_x[far_x.shape[0] - half :], 0)
    put(q ^ 3, far_y[far_y.shape[0] - half :], half)


def assemble(*pieces):
    rows = pieces[0].shape[0]
    return pl.pallas_call(
        assemble_kernel,
        out_shape=jax.ShapeDtypeStruct((rows, 4 * LANES), BF16),
        in_specs=[VMEM] * 5,
        out_specs=VMEM,
        compiler_params=pltpu.CompilerParams(vmem_limit_bytes=8 * MIB),
        cost_estimate=pl.CostEstimate(flops=0, bytes_accessed=3 * MIB, transcendentals=0),
        name="assemble",
    )(*pieces)


def ring_slot(block):
    z = lax.axis_index("ao")
    return ((z ^ (z >> 1)) - (block ^ (block >> 1))) & 3


def column_block(which, blocks):
    first = lax.axis_index("vir") * blocks
    early, late = ring_slot(first), ring_slot(first + 1)
    swapped = jnp.where(early < late, 0, 1)
    return first + (swapped ^ which)


def fetch(slot, refs, target, sem):
    for s, ref in enumerate(refs):

        def start(ref=ref):
            pltpu.make_async_copy(ref, target, sem).start()

        if len(refs) == 1:
            start()
        else:
            pl.when(slot == s)(start)


def fetched(refs, target, sem):
    pltpu.make_async_copy(refs[0], target, sem).wait()


def first_kernel(n_own, n_shifted, which, blocks, *refs):
    where = refs[:n_shifted]
    shifted = refs[n_shifted : 2 * n_shifted]
    own = refs[2 * n_shifted : 2 * n_shifted + n_own]
    other = refs[2 * n_shifted + n_own : 2 * n_shifted + 2 * n_own]
    out, held, total, sems = refs[2 * n_shifted + 2 * n_own :]
    slot = ring_slot(column_block(which, blocks)) if n_own > 1 else 0
    fetch(slot, own, held.at[0], sems.at[0])
    fetch(slot, other, held.at[1], sems.at[1])
    total[...] = jnp.zeros_like(total)
    fetched(own, held.at[0], sems.at[0])
    fetched(other, held.at[1], sems.at[1])
    for there, tiles in zip(where, shifted):

        def add(i, carry, there=there, tiles=tiles):
            sums = []
            for u in range(UNROLL):
                n = i * UNROLL + u
                base_k = pl.multiple_of(there[1, n], LANES)
                window = held[there[2, n], pl.ds(base_k, COLS_WIN), :]
                sums.append((n, jnp.dot(tiles[n], window, preferred_element_type=F32)))
            for n, value in sums:
                base_m = pl.multiple_of(there[0, n], 16)
                total[pl.ds(base_m, ROWS_WIN), :] += value
            return carry

        lax.fori_loop(0, tiles.shape[0] // UNROLL, add, 0)
    out[...] = total[: out.shape[0], :].astype(BF16)


def first_product(where, shifted, own, other, which, blocks):
    rows, width = own[0].shape
    n_tiles = sum(t.shape[0] for t in shifted)
    count = len(shifted)
    return pl.pallas_call(
        functools.partial(first_kernel, len(own), count, which, blocks),
        out_shape=jax.ShapeDtypeStruct((rows, width), BF16),
        in_specs=[SMEM] * count + [VMEM] * count + [ANY] * (2 * len(own)),
        out_specs=VMEM,
        scratch_shapes=[
            pltpu.VMEM((2, rows, width), BF16),
            pltpu.VMEM((rows + TILE, width), F32),
            pltpu.SemaphoreType.DMA((2,)),
        ],
        compiler_params=pltpu.CompilerParams(vmem_limit_bytes=16 * MIB),
        cost_estimate=pl.CostEstimate(
            flops=n_tiles * 4 * ROWS_WIN * COLS_WIN * width, bytes_accessed=6 * MIB,
            transcendentals=0,
        ),
        name="first_product",
    )(*where, *shifted, *own, *other)


def second_kernel(which, blocks, n_before, *refs):
    pair_occ, eps_occ, eps_vir, middle, middle_other = refs[:5]
    own, other = refs[5 : 5 + GROUPS], refs[5 + GROUPS : 5 + 2 * GROUPS]
    out, held, ready, sems, out_sems = refs[5 + 2 * GROUPS + n_before :]
    core = lax.axis_index("rep")
    rows, width = own[0].shape
    columns = middle.shape[1]
    if blocks > 1:
        block = column_block(which, blocks)
        column = pl.multiple_of((block - lax.axis_index("vir") * blocks) * columns, LANES)
        column_energy = pl.multiple_of(block * columns, LANES)
    else:
        column, column_energy = 0, pl.multiple_of(lax.axis_index("vir") * columns, LANES)
    mine = GROUPS // 2

    def load(i):
        wanted = core * mine + i
        slot = ring_slot(wanted) if blocks > 1 else wanted
        fetch(slot, own, held.at[i, 0], sems.at[i, 0])
        fetch(slot, other, held.at[i, 1], sems.at[i, 1])

    load(0)
    energy = eps_occ[pair_occ[0, 0]] + eps_occ[pair_occ[0, 1]]
    by_column = energy - eps_vir[:, pl.ds(column_energy, columns)]
    dims = (((0,), (0,)), ((), ()))
    stores = []
    for i in range(mine):
        first = core * mine * width + i * width
        tall = [
            jnp.transpose(
                jnp.broadcast_to(
                    eps_vir[:, pl.ds(pl.multiple_of(first + k * LANES, LANES), LANES)],
                    (LANES, LANES),
                )
            )
            for k in range(width // LANES)
        ]
        tall = jnp.concatenate(tall, axis=0)
        tall = jnp.concatenate([tall] * (columns // LANES), axis=1)
        fetched(own, held.at[i, 0], sems.at[i, 0])
        if i + 1 < mine:
            load(i + 1)
        total = lax.dot_general(held[i, 0], middle[...], dims, preferred_element_type=F32)
        fetched(other, held.at[i, 1], sems.at[i, 1])
        total += lax.dot_general(held[i, 1], middle_other[...], dims, preferred_element_type=F32)
        ready[i] = (total / (by_column - tall)).astype(BF16)
        store = pltpu.make_async_copy(
            ready.at[i], out.at[0, pl.ds(i * width, width), pl.ds(column, columns)], out_sems.at[i]
        )
        store.start()
        stores.append(store)
    for store in stores:
        store.wait()


def second_product(which, blocks, pair_occ, eps_occ, eps_vir, middle, groups, others, before):
    rows, width = groups[0].shape
    columns = middle[0].shape[1]
    extra = [] if before is None else [before]
    fixed = [pair_occ, eps_occ, eps_vir, *middle, *groups, *others]
    mine = GROUPS // 2
    return pl.pallas_call(
        functools.partial(second_kernel, which, blocks, len(extra)),
        out_shape=jax.ShapeDtypeStruct((1, mine * width, blocks * columns), BF16),
        in_specs=[SMEM] * 2 + [VMEM] * 3 + [ANY] * (2 * GROUPS + len(extra)),
        out_specs=ANY,
        scratch_shapes=[
            pltpu.VMEM((mine, 2, rows, width), BF16),
            pltpu.VMEM((mine, width, columns), BF16),
            pltpu.SemaphoreType.DMA((mine, 2)),
            pltpu.SemaphoreType.DMA((mine,)),
        ],
        input_output_aliases={len(fixed): 0} if extra else {},
        compiler_params=pltpu.CompilerParams(vmem_limit_bytes=20 * MIB),
        cost_estimate=pl.CostEstimate(
            flops=4 * mine * rows * width * columns, bytes_accessed=10 * MIB, transcendentals=0
        ),
        name="second_product",
    )(*fixed, *extra)


def ring_pairs(distance):
    return [(RING[i], RING[(i + distance) % 4]) for i in range(4)]


def other_core(value):
    return lax.ppermute(value, "rep", SWAP)


def to_x(value):
    return lax.ppermute(value, "vir", SWAP)


def to_y(value):
    return lax.ppermute(value, "grp", SWAP)


def to_z(value, distance=1):
    return lax.ppermute(value, "ao", ring_pairs(distance))


def exchange_small(half_ints, coeff, shift):
    z, x, y = lax.axis_index("ao"), lax.axis_index("vir"), lax.axis_index("grp")
    quarter = y * 2 + x
    gray = lambda n: n ^ (n >> 1)
    owner = [gray((gray(z) + k) & 3) for k in range(4)]
    rows = coeff.shape[0]
    half = rows // 2
    together = lax.optimization_barrier
    join = lambda a, b: jnp.concatenate([a, b], axis=0)

    own = lax.dynamic_slice_in_dim(coeff, quarter * LANES, LANES, 1)
    t = [
        lax.dynamic_index_in_dim(half_ints[:, 0], owner[k], 0, False) for k in range(4)
    ]
    z1, t = together((to_z(own), t))
    x1, y1, z2, t = together((to_x(z1), to_y(z1), to_z(z1), t))
    x2, y2, z3, t1, t = together(
        (to_x(join(z2, y1[:half])), to_y(join(z2, x1[half:])), to_z(z2), to_z(t[1], 1), t)
    )
    group1 = assemble(z1, x1, y1, x2, y2)
    x3, y3, t2, t3, group1, early = together(
        (
            to_x(join(z3, y2[:half])), to_y(join(z3, x2[half:rows])),
            to_z(t[2], 2), to_z(t[3], 3), group1, shift((0, 1), [t[0], t1]),
        )
    )
    group2 = assemble(z2, x2, y2, x3, y3)
    x4, y4, late = together((to_x(y3[:half]), to_y(x3[half:rows]), shift((2, 3), [t2, t3])))
    group3 = assemble(z3, x3, y3, x4, y4)
    return [coeff, group1, group2, group3], [early, late]


def exchange_any(half_ints, coeff):
    count = lax.axis_size("ao")
    gathered = lax.all_gather(coeff, "ao", axis=1, tiled=True)
    width = gathered.shape[1] // GROUPS
    tiles = lax.all_to_all(half_ints, "ao", split_axis=0, concat_axis=2, tiled=True)[0, 0]
    groups = [gathered[:, g * width : (g + 1) * width] for g in range(GROUPS)]
    return gathered, groups, tiles


def local(half_ints, coeff, eps_occ, eps_vir, pair_occ, tile_list, shell_extra):
    sizes = tuple(lax.axis_size(name) for name in ("grp", "ao", "vir"))
    rows, width = coeff.shape
    full_width = width * sizes[1]
    b_width = full_width // sizes[2]
    vir = lax.axis_index("vir")
    ringed = sizes == (2, 4, 2) and width == 4 * LANES
    shift = lambda slots, tiles: shift_tiles(slots, tile_list, shell_extra, tiles, rows)
    if ringed:
        groups, moved = exchange_small(half_ints, coeff, shift)
        own, blocks = groups, b_width // width
    else:
        gathered, groups, tiles = exchange_any(half_ints, coeff)
        own, blocks = [lax.dynamic_slice_in_dim(gathered, vir * b_width, b_width, 1)], 1
        moved = [shift((None,), [tiles])]
    others = [other_core(g) for g in groups]
    other = others if ringed else [other_core(own[0])]
    shifted, where = [m[0] for m in moved], [m[1] for m in moved]
    energies = eps_vir.reshape(1, -1)
    out = None
    for which in range(blocks):
        middle = first_product(where, shifted, own, other, which, blocks)
        middle, where, shifted = lax.optimization_barrier((middle, where, shifted))
        both = (middle, other_core(middle))
        out = second_product(
            which, blocks, pair_occ, eps_occ, energies, both, groups, others, out
        )
    return out


def solution(mesh):
    in_specs = (
        P("grp", "rep", "ao", None, None),
        P("rep", "ao"),
        P(),
        P(),
        P(("grp", "ao"), None),
        P("rep", None, None),
        P(),
    )
    out_specs = P(("grp", "ao"), "rep", "vir")
    return jax.shard_map(local, mesh=mesh, in_specs=in_specs, out_specs=out_specs, check_vma=False)
```

```python
import functools

import jax
import jax.numpy as jnp
from jax import lax
from jax.experimental import pallas as pl
from jax.experimental.pallas import tpu as pltpu
from jax.sharding import PartitionSpec as P

TILE = 128
HALF_BLK = 12
LANES = 128
ROWS_WIN = 144
COLS_WIN = 256
GROUPS = 4
UNROLL = 6
SHIFT_UNROLL = 3
RING = (0, 1, 3, 2)
SWAP = ((0, 1), (1, 0))
F32 = jnp.float32
BF16 = jnp.bfloat16
SMEM = pl.BlockSpec(memory_space=pltpu.SMEM)
VMEM = pl.BlockSpec(memory_space=pltpu.VMEM)
ANY = pl.BlockSpec(memory_space=pl.ANY)
MIB = 1 << 20


def ring_group(step):
    z = lax.axis_index("ao")
    spot = ((z ^ (z >> 1)) - step) & 3
    return spot ^ (spot >> 1)


def plan_kernel(slots, count, rows_half, a_width, listed, extra, pair_occ, eps_occ, eps_vir, plan, by_col, by_row, offsets):
    core = lax.axis_index("rep")

    def lay(k, start):
        start = jnp.where(k == HALF_BLK, 0, start)
        offsets[k] = start
        return start + TILE // 2 + extra[k // HALF_BLK, lax.rem(k, HALF_BLK)]

    lax.fori_loop(0, 2 * HALF_BLK, lay, jnp.int32(0))
    for r, slot in enumerate(slots):
        first = 0 if slot is None else ring_group(slot) * count

        def one(i, carry, r=r, first=first):
            m = listed[0, first + i, 0]
            k = listed[0, first + i, 1]
            half_k = k // HALF_BLK
            off_m = offsets[core * HALF_BLK + m]
            off_k = offsets[k]
            base_m = (off_m // 16) * 16
            base_k = jnp.minimum((off_k // LANES) * LANES, rows_half - COLS_WIN)
            at = r * count + i
            plan[0, at] = base_m
            plan[1, at] = base_k
            plan[2, at] = jnp.where(half_k == core, 0, 1)
            plan[3, at] = off_m - base_m
            plan[4, at] = off_k - base_k
            plan[5, at] = TILE // 2 + extra[core, m]
            plan[6, at] = TILE // 2 + extra[half_k, lax.rem(k, HALF_BLK)]
            return carry

        lax.fori_loop(0, count, one, 0)
    energy = eps_occ[pair_occ[0, 0]] + eps_occ[pair_occ[0, 1]]
    columns = by_col.shape[1]
    start = pl.multiple_of(lax.axis_index("vir") * columns, LANES)
    by_col[...] = energy - eps_vir[:, pl.ds(start, columns)]
    for k in range(a_width // LANES):
        start = pl.multiple_of(core * a_width + k * LANES, LANES)
        row = jnp.broadcast_to(eps_vir[:, pl.ds(start, LANES)], (LANES, LANES))
        by_row[k * LANES : (k + 1) * LANES, :] = jnp.transpose(row)


def make_plan(slots, listed, shell_extra, pair_occ, eps_occ, eps_vir, rows_half, a_width, b_width):
    total = listed.shape[1]
    return pl.pallas_call(
        functools.partial(plan_kernel, slots, total // len(slots), rows_half, a_width),
        out_shape=(
            jax.ShapeDtypeStruct((7, total), jnp.int32),
            jax.ShapeDtypeStruct((1, b_width), F32),
            jax.ShapeDtypeStruct((a_width, LANES), F32),
        ),
        in_specs=[SMEM] * 4 + [VMEM],
        out_specs=(SMEM, VMEM, VMEM),
        scratch_shapes=[pltpu.SMEM((2 * HALF_BLK,), jnp.int32)],
        compiler_params=pltpu.CompilerParams(vmem_limit_bytes=6 * MIB),
        cost_estimate=pl.CostEstimate(flops=0, bytes_accessed=2 * MIB, transcendentals=0),
        name="make_plan",
    )(listed, shell_extra, pair_occ, eps_occ, eps_vir)


def shift_loop(plan, first, held, shifted):
    down_from = lax.broadcasted_iota(jnp.int32, (ROWS_WIN, TILE), 1)
    down = lax.broadcasted_iota(jnp.int32, (ROWS_WIN, TILE), 0) - down_from
    right_from = lax.broadcasted_iota(jnp.int32, (TILE, COLS_WIN), 0)
    right = lax.broadcasted_iota(jnp.int32, (TILE, COLS_WIN), 1) - right_from

    def some(group, carry):
        moved = []
        for u in range(SHIFT_UNROLL):
            i = group * SHIFT_UNROLL + u
            at = first + i
            take_m = jnp.where((down == plan[3, at]) & (down_from < plan[5, at]), 1.0, 0.0)
            take_k = jnp.where((right == plan[4, at]) & (right_from < plan[6, at]), 1.0, 0.0)
            value = jnp.dot(take_m.astype(BF16), held[i], preferred_element_type=F32)
            moved.append((i, value.astype(BF16), take_k.astype(BF16)))
        for i, value, take_k in moved:
            value = jnp.dot(value, take_k, preferred_element_type=F32)
            shifted[i] = value.astype(BF16)
        return carry

    lax.fori_loop(0, held.shape[0] // SHIFT_UNROLL, some, 0)


def tile_copies(tiles, held, sems):
    count = tiles[0].shape[0]
    return [
        pltpu.make_async_copy(ref, held.at[pl.ds(r * count, count)], sems.at[r])
        for r, ref in enumerate(tiles)
    ]


def shift_kernel(first, n_refs, *refs):
    plan = refs[0]
    tiles = refs[1 : 1 + n_refs]
    shifted, held, sems = refs[1 + n_refs :]
    copies = tile_copies(tiles, held, sems)
    for copy in copies:
        copy.start()
    for copy in copies:
        copy.wait()
    shift_loop(plan, first, held, shifted)


def shift_tiles(plan, first, tiles):
    total = sum(t.shape[0] for t in tiles)
    return pl.pallas_call(
        functools.partial(shift_kernel, first, len(tiles)),
        out_shape=jax.ShapeDtypeStruct((total, ROWS_WIN, COLS_WIN), BF16),
        in_specs=[SMEM] + [ANY] * len(tiles),
        out_specs=VMEM,
        scratch_shapes=[
            pltpu.VMEM((total, TILE, TILE), BF16),
            pltpu.SemaphoreType.DMA((len(tiles),)),
        ],
        compiler_params=pltpu.CompilerParams(vmem_limit_bytes=14 * MIB),
        cost_estimate=pl.CostEstimate(flops=0, bytes_accessed=8 * MIB, transcendentals=0),
        name="shift_tiles",
    )(plan, *tiles)


def stay_kernel(value, out):
    out[...] = value[...]


def stay(value):
    return pl.pallas_call(
        stay_kernel,
        out_shape=jax.ShapeDtypeStruct(value.shape, value.dtype),
        in_specs=[VMEM],
        out_specs=VMEM,
        compiler_params=pltpu.CompilerParams(vmem_limit_bytes=8 * MIB),
        cost_estimate=pl.CostEstimate(flops=0, bytes_accessed=3 * MIB, transcendentals=0),
        name="stay",
    )(value)


def assemble_kernel(own, by_x, by_y, far_x, far_y, out, sems):
    rows = own.shape[0]
    half = rows // 2
    q = lax.axis_index("grp") * 2 + lax.axis_index("vir")
    parts = (
        (own, 0, rows, q, 0),
        (by_x, 0, rows, q ^ 1, 0),
        (by_y, 0, rows, q ^ 2, 0),
        (far_x, far_x.shape[0] - half, half, q ^ 3, 0),
        (far_y, far_y.shape[0] - half, half, q ^ 3, half),
    )
    copies = []
    for piece, start, count, at, first in parts:
        lanes = pl.ds(pl.multiple_of(at * LANES, LANES), LANES)
        copies.append(
            pltpu.make_async_copy(
                piece.at[pl.ds(start, count)], out.at[pl.ds(first, count), lanes],
                sems.at[len(copies)],
            )
        )
    for copy in copies:
        copy.start()
    for copy in copies:
        copy.wait()


def assemble(*pieces):
    rows = pieces[0].shape[0]
    return pl.pallas_call(
        assemble_kernel,
        out_shape=jax.ShapeDtypeStruct((rows, 4 * LANES), BF16),
        in_specs=[ANY] * 5,
        out_specs=VMEM,
        scratch_shapes=[pltpu.SemaphoreType.DMA((5,))],
        compiler_params=pltpu.CompilerParams(vmem_limit_bytes=8 * MIB),
        cost_estimate=pl.CostEstimate(flops=0, bytes_accessed=3 * MIB, transcendentals=0),
        name="assemble",
    )(*pieces)


def ring_slot(block):
    z = lax.axis_index("ao")
    return ((z ^ (z >> 1)) - (block ^ (block >> 1))) & 3


def column_block(which, blocks):
    first = lax.axis_index("vir") * blocks
    early, late = ring_slot(first), ring_slot(first + 1)
    swapped = jnp.where(early < late, 0, 1)
    return first + (swapped ^ which)


def pick(slot, first, refs, target):
    for s, ref in enumerate(refs):

        def copy(ref=ref):
            target[...] = ref[...]

        if len(refs) == 1:
            copy()
        else:
            pl.when(slot == first + s)(copy)


def first_kernel(n_own, n_shifted, n_late, which, blocks, *refs):
    plan = refs[0]
    shifted = list(refs[1 : 1 + n_shifted])
    late = refs[1 + n_shifted : 1 + n_shifted + n_late]
    refs = refs[1 + n_shifted + n_late :]
    own, other = refs[:n_own], refs[n_own : 2 * n_own]
    out = refs[2 * n_own]
    refs = refs[2 * n_own + 1 :]
    if n_late:
        late_shifted, held, total, late_held, sems = refs
        copies = tile_copies(late, late_held, sems)
        for copy in copies:
            copy.start()
    else:
        held, total = refs
    slot = ring_slot(column_block(which, blocks)) if n_own > 1 else 0
    pick(slot, which, own, held.at[0])
    pick(slot, which, other, held.at[1])
    total[...] = jnp.zeros_like(total)
    if n_late:
        for copy in copies:
            copy.wait()
        shift_loop(plan, sum(t.shape[0] for t in shifted), late_held, late_shifted)
        shifted.append(late_shifted)
    before = 0
    for tiles in shifted:

        def add(i, carry, before=before, tiles=tiles):
            sums = []
            for u in range(UNROLL):
                n = i * UNROLL + u
                base_k = pl.multiple_of(plan[1, before + n], LANES)
                window = held[plan[2, before + n], pl.ds(base_k, COLS_WIN), :]
                sums.append((n, jnp.dot(tiles[n], window, preferred_element_type=F32)))
            for n, value in sums:
                base_m = pl.multiple_of(plan[0, before + n], 16)
                total[pl.ds(base_m, ROWS_WIN), :] += value
            return carry

        lax.fori_loop(0, tiles.shape[0] // UNROLL, add, 0)
        before += tiles.shape[0]
    out[...] = total[: out.shape[0], :].astype(BF16)


def first_product(plan, shifted, late, own, other, which, blocks):
    rows, width = own[0].shape
    n_tiles = plan.shape[1]
    n_late = sum(t.shape[0] for t in late)
    out_shape = [jax.ShapeDtypeStruct((rows, width), BF16)]
    scratch = [
        pltpu.VMEM((2, rows, width), BF16),
        pltpu.VMEM((rows + TILE, width), F32),
    ]
    if late:
        out_shape.append(jax.ShapeDtypeStruct((n_late, ROWS_WIN, COLS_WIN), BF16))
        scratch += [
            pltpu.VMEM((n_late, TILE, TILE), BF16),
            pltpu.SemaphoreType.DMA((len(late),)),
        ]
    result = pl.pallas_call(
        functools.partial(first_kernel, len(own), len(shifted), len(late), which, blocks),
        out_shape=out_shape,
        in_specs=[SMEM] + [VMEM] * len(shifted) + [ANY] * len(late) + [VMEM] * (2 * len(own)),
        out_specs=[VMEM] * len(out_shape),
        scratch_shapes=scratch,
        compiler_params=pltpu.CompilerParams(vmem_limit_bytes=14 * MIB),
        cost_estimate=pl.CostEstimate(
            flops=n_tiles * 4 * ROWS_WIN * COLS_WIN * width, bytes_accessed=6 * MIB,
            transcendentals=0,
        ),
        name="first_product",
    )(plan, *shifted, *late, *own, *other)
    return result[0], [*shifted, *result[1:]]


def second_kernel(which, blocks, n_groups, n_before, *refs):
    by_col, by_row, middle, middle_other = refs[:4]
    core = lax.axis_index("rep")
    mine = GROUPS // 2
    if n_groups:
        own, other = refs[4 : 4 + GROUPS], refs[4 + GROUPS : 4 + 2 * GROUPS]
        out, held, ready, out_sems = refs[4 + 2 * GROUPS + n_before :]
        for i in range(mine):
            wanted = core * mine + i
            slot = ring_slot(wanted) if blocks > 1 else wanted
            pick(slot, 0, own, held.at[i, 0])
            pick(slot, 0, other, held.at[i, 1])
    else:
        held = refs[4]
        out, ready, out_sems = refs[5 + n_before :]
    width = held.shape[3]
    columns = middle.shape[1]
    if blocks > 1:
        block = column_block(which, blocks) - lax.axis_index("vir") * blocks
        column = pl.multiple_of(block * columns, LANES)
    else:
        column = 0
    dims = (((0,), (0,)), ((), ()))
    stores = []
    for i in range(mine):
        total = lax.dot_general(held[i, 0], middle[...], dims, preferred_element_type=F32)
        total += lax.dot_general(held[i, 1], middle_other[...], dims, preferred_element_type=F32)
        tall = by_row[i * width : (i + 1) * width, :]
        tall = jnp.concatenate([tall] * (columns // LANES), axis=1)
        ready[i] = (total / (by_col[:, pl.ds(column, columns)] - tall)).astype(BF16)
        store = pltpu.make_async_copy(
            ready.at[i], out.at[0, pl.ds(i * width, width), pl.ds(column, columns)], out_sems.at[i]
        )
        store.start()
        stores.append(store)
    for store in stores:
        store.wait()


def second_product(which, blocks, energies, middle, groups, held, before):
    rows, columns = middle[0].shape
    mine = GROUPS // 2
    width = energies[1].shape[0] // mine
    extra = [] if before is None else [before]
    fixed = [*energies, *middle, *(groups if held is None else [held])]
    out_shape = [jax.ShapeDtypeStruct((1, mine * width, blocks * columns), BF16)]
    out_specs = [ANY]
    if held is None:
        out_shape.append(jax.ShapeDtypeStruct((mine, 2, rows, width), BF16))
        out_specs.append(VMEM)
    result = pl.pallas_call(
        functools.partial(
            second_kernel, which, blocks, len(groups) if held is None else 0, len(extra)
        ),
        out_shape=out_shape,
        in_specs=[VMEM] * len(fixed) + [ANY] * len(extra),
        out_specs=out_specs,
        scratch_shapes=[
            pltpu.VMEM((mine, width, columns), BF16),
            pltpu.SemaphoreType.DMA((mine,)),
        ],
        input_output_aliases={len(fixed): 0} if extra else {},
        compiler_params=pltpu.CompilerParams(vmem_limit_bytes=16 * MIB),
        cost_estimate=pl.CostEstimate(
            flops=4 * mine * rows * width * columns, bytes_accessed=10 * MIB, transcendentals=0
        ),
        name="second_product",
    )(*fixed, *extra)
    return (result[0], result[1] if held is None else held)


def ring_pairs(distance):
    return [(RING[i], RING[(i + distance) % 4]) for i in range(4)]


def other_core(value):
    return lax.ppermute(value, "rep", SWAP)


def to_x(value):
    return lax.ppermute(value, "vir", SWAP)


def to_y(value):
    return lax.ppermute(value, "grp", SWAP)


def to_z(value, distance=1):
    return lax.ppermute(value, "ao", ring_pairs(distance))


def exchange_small(half_ints, coeff, plan, shift):
    z, x, y = lax.axis_index("ao"), lax.axis_index("vir"), lax.axis_index("grp")
    quarter = y * 2 + x
    gray = lambda n: n ^ (n >> 1)
    owner = [gray((gray(z) + k) & 3) for k in range(4)]
    rows = coeff.shape[0]
    half = rows // 2
    together = lax.optimization_barrier
    join = lambda a, b: jnp.concatenate([a, b], axis=0)

    own = lax.dynamic_slice_in_dim(coeff, quarter * LANES, LANES, 1)
    t = [
        lax.dynamic_index_in_dim(half_ints[:, 0], owner[k], 0, False) for k in range(4)
    ]
    z1, t, group0 = together((to_z(own), t, stay(coeff)))
    x1, y1, z2, t, plan = together((to_x(z1), to_y(z1), to_z(z1), t, plan))
    x2, y2, z3, t1, t = together(
        (to_x(join(z2, y1[:half])), to_y(join(z2, x1[half:])), to_z(z2), to_z(t[1], 1), t)
    )
    group1 = assemble(z1, x1, y1, x2, y2)
    early = shift(plan, 0, [t[0], t1])
    early, last = together((early, t[2]))
    t2, t3 = to_z(last, 2), to_z(t[3], 3)
    x3, y3, group1, early = together(
        (to_x(join(z3, y2[:half])), to_y(join(z3, x2[half:rows])), group1, early)
    )
    group2 = assemble(z2, x2, y2, x3, y3)
    late = shift(plan, 2 * t2.shape[0], [t2, t3])
    x4, y4, late = together((to_x(y3[:half]), to_y(x3[half:rows]), late))
    group3 = assemble(z3, x3, y3, x4, y4)
    return [group0, group1, group2, group3], [early, late], [], plan


def exchange_any(half_ints, coeff):
    count = lax.axis_size("ao")
    gathered = lax.all_gather(coeff, "ao", axis=1, tiled=True)
    width = gathered.shape[1] // GROUPS
    tiles = lax.all_to_all(half_ints, "ao", split_axis=0, concat_axis=2, tiled=True)[0, 0]
    groups = [gathered[:, g * width : (g + 1) * width] for g in range(GROUPS)]
    return gathered, groups, tiles


def local(half_ints, coeff, eps_occ, eps_vir, pair_occ, tile_list, shell_extra):
    sizes = tuple(lax.axis_size(name) for name in ("grp", "ao", "vir"))
    rows, width = coeff.shape
    full_width = width * sizes[1]
    b_width = full_width // sizes[2]
    vir = lax.axis_index("vir")
    ringed = sizes == (2, 4, 2) and width == 4 * LANES
    plan, *energies = make_plan(
        tuple(range(4)) if ringed else (None,), tile_list, shell_extra, pair_occ, eps_occ,
        eps_vir.reshape(1, -1), rows, full_width // lax.axis_size("rep"), b_width,
    )
    if ringed:
        groups, shifted, late, plan = exchange_small(half_ints, coeff, plan, shift_tiles)
        own, blocks = groups, b_width // width
    else:
        gathered, groups, tiles = exchange_any(half_ints, coeff)
        own, blocks = [lax.dynamic_slice_in_dim(gathered, vir * b_width, b_width, 1)], 1
        shifted, late = [shift_tiles(plan, 0, [tiles])], []
    others = [other_core(g) for g in groups]
    other = others if ringed else [other_core(own[0])]
    out = held = None
    for which in range(blocks):
        some = slice(which, GROUPS - 1 + which) if ringed else slice(None)
        middle, shifted = first_product(
            plan, shifted, late, own[some], other[some], which, blocks
        )
        middle, shifted = lax.optimization_barrier((middle, shifted))
        late = []
        both = (middle, other_core(middle))
        out, held = second_product(
            which, blocks, energies, both, [*groups, *others], held, out
        )
    return out


def solution(mesh):
    in_specs = (
        P("grp", "rep", "ao", None, None),
        P("rep", "ao"),
        P(),
        P(),
        P(("grp", "ao"), None),
        P("rep", None, None),
        P(),
    )
    out_specs = P(("grp", "ao"), "rep", "vir")
    return jax.shard_map(local, mesh=mesh, in_specs=in_specs, out_specs=out_specs, check_vma=False)
```

```python
import functools

import jax
import jax.numpy as jnp
from jax import lax
from jax.experimental import pallas as pl
from jax.experimental.pallas import tpu as pltpu
from jax.sharding import PartitionSpec as P

TILE = 128
HALF_BLK = 12
LANES = 128
ROWS_WIN = 144
COLS_WIN = 256
GROUPS = 4
UNROLL = 12
SHIFT_UNROLL = 6
RING = (0, 1, 3, 2)
SWAP = ((0, 1), (1, 0))
F32 = jnp.float32
BF16 = jnp.bfloat16
SMEM = pl.BlockSpec(memory_space=pltpu.SMEM)
VMEM = pl.BlockSpec(memory_space=pltpu.VMEM)
ANY = pl.BlockSpec(memory_space=pl.ANY)
MIB = 1 << 20


def ring_group(step):
    z = lax.axis_index("ao")
    spot = ((z ^ (z >> 1)) - step) & 3
    return spot ^ (spot >> 1)


def plan_kernel(slots, count, rows_half, a_width, listed, extra, pair_occ, eps_occ, eps_vir, plan, by_col, by_row, offsets):
    core = lax.axis_index("rep")

    def lay(k, start):
        start = jnp.where(k == HALF_BLK, 0, start)
        offsets[k] = start
        return start + TILE // 2 + extra[k // HALF_BLK, lax.rem(k, HALF_BLK)]

    lax.fori_loop(0, 2 * HALF_BLK, lay, jnp.int32(0))
    for r, slot in enumerate(slots):
        first = 0 if slot is None else ring_group(slot) * count

        def one(i, carry, r=r, first=first):
            m = listed[0, first + i, 0]
            k = listed[0, first + i, 1]
            half_k = k // HALF_BLK
            off_m = offsets[core * HALF_BLK + m]
            off_k = offsets[k]
            base_m = (off_m // 16) * 16
            base_k = jnp.minimum((off_k // LANES) * LANES, rows_half - COLS_WIN)
            at = r * count + i
            plan[0, at] = base_m
            plan[1, at] = base_k
            plan[2, at] = jnp.where(half_k == core, 0, 1)
            plan[3, at] = off_m - base_m
            plan[4, at] = off_k - base_k
            plan[5, at] = TILE // 2 + extra[core, m]
            plan[6, at] = TILE // 2 + extra[half_k, lax.rem(k, HALF_BLK)]
            return carry

        lax.fori_loop(0, count, one, 0)
    energy = eps_occ[pair_occ[0, 0]] + eps_occ[pair_occ[0, 1]]
    columns = by_col.shape[1]
    start = pl.multiple_of(lax.axis_index("vir") * columns, LANES)
    by_col[...] = energy - eps_vir[:, pl.ds(start, columns)]
    for k in range(a_width // LANES):
        start = pl.multiple_of(core * a_width + k * LANES, LANES)
        row = jnp.broadcast_to(eps_vir[:, pl.ds(start, LANES)], (LANES, LANES))
        by_row[k * LANES : (k + 1) * LANES, :] = jnp.transpose(row)


def make_plan(slots, listed, shell_extra, pair_occ, eps_occ, eps_vir, rows_half, a_width, b_width):
    total = listed.shape[1]
    return pl.pallas_call(
        functools.partial(plan_kernel, slots, total // len(slots), rows_half, a_width),
        out_shape=(
            jax.ShapeDtypeStruct((7, total), jnp.int32),
            jax.ShapeDtypeStruct((1, b_width), F32),
            jax.ShapeDtypeStruct((a_width, LANES), F32),
        ),
        in_specs=[SMEM] * 4 + [VMEM],
        out_specs=(SMEM, VMEM, VMEM),
        scratch_shapes=[pltpu.SMEM((2 * HALF_BLK,), jnp.int32)],
        compiler_params=pltpu.CompilerParams(vmem_limit_bytes=6 * MIB),
        cost_estimate=pl.CostEstimate(flops=0, bytes_accessed=2 * MIB, transcendentals=0),
        name="make_plan",
    )(listed, shell_extra, pair_occ, eps_occ, eps_vir)


def shift_loop(plan, first, held, shifted):
    down_from = lax.broadcasted_iota(jnp.int32, (ROWS_WIN, TILE), 1)
    down = lax.broadcasted_iota(jnp.int32, (ROWS_WIN, TILE), 0) - down_from
    right_from = lax.broadcasted_iota(jnp.int32, (TILE, COLS_WIN), 0)
    right = lax.broadcasted_iota(jnp.int32, (TILE, COLS_WIN), 1) - right_from

    def some(group, carry):
        moved = []
        for u in range(SHIFT_UNROLL):
            i = group * SHIFT_UNROLL + u
            at = first + i
            take_m = jnp.where((down == plan[3, at]) & (down_from < plan[5, at]), 1.0, 0.0)
            take_k = jnp.where((right == plan[4, at]) & (right_from < plan[6, at]), 1.0, 0.0)
            value = jnp.dot(take_m.astype(BF16), held[i], preferred_element_type=F32)
            moved.append((i, value.astype(BF16), take_k.astype(BF16)))
        for i, value, take_k in moved:
            value = jnp.dot(value, take_k, preferred_element_type=F32)
            shifted[i] = value.astype(BF16)
        return carry

    lax.fori_loop(0, held.shape[0] // SHIFT_UNROLL, some, 0)


def tile_copies(tiles, held, sems):
    count = tiles[0].shape[0]
    return [
        pltpu.make_async_copy(ref, held.at[pl.ds(r * count, count)], sems.at[r])
        for r, ref in enumerate(tiles)
    ]


def shift_kernel(first, n_refs, *refs):
    plan = refs[0]
    tiles = refs[1 : 1 + n_refs]
    shifted, held, sems = refs[1 + n_refs :]
    copies = tile_copies(tiles, held, sems)
    for copy in copies:
        copy.start()
    for copy in copies:
        copy.wait()
    shift_loop(plan, first, held, shifted)


def shift_tiles(plan, first, tiles):
    total = sum(t.shape[0] for t in tiles)
    return pl.pallas_call(
        functools.partial(shift_kernel, first, len(tiles)),
        out_shape=jax.ShapeDtypeStruct((total, ROWS_WIN, COLS_WIN), BF16),
        in_specs=[SMEM] + [ANY] * len(tiles),
        out_specs=VMEM,
        scratch_shapes=[
            pltpu.VMEM((total, TILE, TILE), BF16),
            pltpu.SemaphoreType.DMA((len(tiles),)),
        ],
        compiler_params=pltpu.CompilerParams(vmem_limit_bytes=14 * MIB),
        cost_estimate=pl.CostEstimate(flops=0, bytes_accessed=8 * MIB, transcendentals=0),
        name="shift_tiles",
    )(plan, *tiles)


def stay_kernel(value, out):
    out[...] = value[...]


def stay(value):
    return pl.pallas_call(
        stay_kernel,
        out_shape=jax.ShapeDtypeStruct(value.shape, value.dtype),
        in_specs=[VMEM],
        out_specs=VMEM,
        compiler_params=pltpu.CompilerParams(vmem_limit_bytes=8 * MIB),
        cost_estimate=pl.CostEstimate(flops=0, bytes_accessed=3 * MIB, transcendentals=0),
        name="stay",
    )(value)


def assemble_kernel(own, by_x, by_y, far_x, far_y, out, sems):
    rows = own.shape[0]
    half = rows // 2
    q = lax.axis_index("grp") * 2 + lax.axis_index("vir")
    parts = (
        (own, 0, rows, q, 0),
        (by_x, 0, rows, q ^ 1, 0),
        (by_y, 0, rows, q ^ 2, 0),
        (far_x, far_x.shape[0] - half, half, q ^ 3, 0),
        (far_y, far_y.shape[0] - half, half, q ^ 3, half),
    )
    copies = []
    for piece, start, count, at, first in parts:
        lanes = pl.ds(pl.multiple_of(at * LANES, LANES), LANES)
        copies.append(
            pltpu.make_async_copy(
                piece.at[pl.ds(start, count)], out.at[pl.ds(first, count), lanes],
                sems.at[len(copies)],
            )
        )
    for copy in copies:
        copy.start()
    for copy in copies:
        copy.wait()


def assemble(*pieces):
    rows = pieces[0].shape[0]
    return pl.pallas_call(
        assemble_kernel,
        out_shape=jax.ShapeDtypeStruct((rows, 4 * LANES), BF16),
        in_specs=[ANY] * 5,
        out_specs=VMEM,
        scratch_shapes=[pltpu.SemaphoreType.DMA((5,))],
        compiler_params=pltpu.CompilerParams(vmem_limit_bytes=8 * MIB),
        cost_estimate=pl.CostEstimate(flops=0, bytes_accessed=3 * MIB, transcendentals=0),
        name="assemble",
    )(*pieces)


def ring_slot(block):
    z = lax.axis_index("ao")
    return ((z ^ (z >> 1)) - (block ^ (block >> 1))) & 3


def column_block(which, blocks):
    first = lax.axis_index("vir") * blocks
    early, late = ring_slot(first), ring_slot(first + 1)
    swapped = jnp.where(early < late, 0, 1)
    return first + (swapped ^ which)


def pick(slot, first, refs, target):
    for s, ref in enumerate(refs):

        def copy(ref=ref):
            target[...] = ref[...]

        if len(refs) == 1:
            copy()
        else:
            pl.when(slot == first + s)(copy)


def first_kernel(n_own, n_shifted, n_late, which, blocks, *refs):
    plan = refs[0]
    shifted = list(refs[1 : 1 + n_shifted])
    late = refs[1 + n_shifted : 1 + n_shifted + n_late]
    refs = refs[1 + n_shifted + n_late :]
    own, other = refs[:n_own], refs[n_own : 2 * n_own]
    out = refs[2 * n_own]
    refs = refs[2 * n_own + 1 :]
    if n_late:
        late_shifted, held, total, late_held, sems = refs
        copies = tile_copies(late, late_held, sems)
        for copy in copies:
            copy.start()
    else:
        held, total = refs
    slot = ring_slot(column_block(which, blocks)) if n_own > 1 else 0
    pick(slot, which, own, held.at[0])
    pick(slot, which, other, held.at[1])
    total[...] = jnp.zeros_like(total)
    if n_late:
        for copy in copies:
            copy.wait()
        shift_loop(plan, sum(t.shape[0] for t in shifted), late_held, late_shifted)
        shifted.append(late_shifted)
    before = 0
    for tiles in shifted:

        def add(i, carry, before=before, tiles=tiles):
            sums = []
            for u in range(UNROLL):
                n = i * UNROLL + u
                base_k = pl.multiple_of(plan[1, before + n], LANES)
                window = held[plan[2, before + n], pl.ds(base_k, COLS_WIN), :]
                sums.append((n, jnp.dot(tiles[n], window, preferred_element_type=F32)))
            for n, value in sums:
                base_m = pl.multiple_of(plan[0, before + n], 16)
                total[pl.ds(base_m, ROWS_WIN), :] += value
            return carry

        lax.fori_loop(0, tiles.shape[0] // UNROLL, add, 0)
        before += tiles.shape[0]
    out[...] = total[: out.shape[0], :].astype(BF16)


def first_product(plan, shifted, late, own, other, which, blocks):
    rows, width = own[0].shape
    n_tiles = plan.shape[1]
    n_late = sum(t.shape[0] for t in late)
    out_shape = [jax.ShapeDtypeStruct((rows, width), BF16)]
    scratch = [
        pltpu.VMEM((2, rows, width), BF16),
        pltpu.VMEM((rows + TILE, width), F32),
    ]
    if late:
        out_shape.append(jax.ShapeDtypeStruct((n_late, ROWS_WIN, COLS_WIN), BF16))
        scratch += [
            pltpu.VMEM((n_late, TILE, TILE), BF16),
            pltpu.SemaphoreType.DMA((len(late),)),
        ]
    result = pl.pallas_call(
        functools.partial(first_kernel, len(own), len(shifted), len(late), which, blocks),
        out_shape=out_shape,
        in_specs=[SMEM] + [VMEM] * len(shifted) + [ANY] * len(late) + [VMEM] * (2 * len(own)),
        out_specs=[VMEM] * len(out_shape),
        scratch_shapes=scratch,
        compiler_params=pltpu.CompilerParams(vmem_limit_bytes=14 * MIB),
        cost_estimate=pl.CostEstimate(
            flops=n_tiles * 4 * ROWS_WIN * COLS_WIN * width, bytes_accessed=6 * MIB,
            transcendentals=0,
        ),
        name="first_product",
    )(plan, *shifted, *late, *own, *other)
    return result[0], [*shifted, *result[1:]]


def second_kernel(which, blocks, n_groups, n_before, *refs):
    by_col, by_row, middle, middle_other = refs[:4]
    core = lax.axis_index("rep")
    mine = GROUPS // 2
    if n_groups:
        own, other = refs[4 : 4 + GROUPS], refs[4 + GROUPS : 4 + 2 * GROUPS]
        out, held, ready, out_sems = refs[4 + 2 * GROUPS + n_before :]
        for i in range(mine):
            wanted = core * mine + i
            slot = ring_slot(wanted) if blocks > 1 else wanted
            pick(slot, 0, own, held.at[i, 0])
            pick(slot, 0, other, held.at[i, 1])
    else:
        held = refs[4]
        out, ready, out_sems = refs[5 + n_before :]
    width = held.shape[3]
    columns = middle.shape[1]
    if blocks > 1:
        block = column_block(which, blocks) - lax.axis_index("vir") * blocks
        column = pl.multiple_of(block * columns, LANES)
    else:
        column = 0
    dims = (((0,), (0,)), ((), ()))
    stores = []
    for i in range(mine):
        total = lax.dot_general(held[i, 0], middle[...], dims, preferred_element_type=F32)
        total += lax.dot_general(held[i, 1], middle_other[...], dims, preferred_element_type=F32)
        tall = by_row[i * width : (i + 1) * width, :]
        tall = jnp.concatenate([tall] * (columns // LANES), axis=1)
        ready[i] = (total / (by_col[:, pl.ds(column, columns)] - tall)).astype(BF16)
        store = pltpu.make_async_copy(
            ready.at[i], out.at[0, pl.ds(i * width, width), pl.ds(column, columns)], out_sems.at[i]
        )
        store.start()
        stores.append(store)
    for store in stores:
        store.wait()


def second_product(which, blocks, energies, middle, groups, held, before):
    rows, columns = middle[0].shape
    mine = GROUPS // 2
    width = energies[1].shape[0] // mine
    extra = [] if before is None else [before]
    fixed = [*energies, *middle, *(groups if held is None else [held])]
    out_shape = [jax.ShapeDtypeStruct((1, mine * width, blocks * columns), BF16)]
    out_specs = [ANY]
    if held is None:
        out_shape.append(jax.ShapeDtypeStruct((mine, 2, rows, width), BF16))
        out_specs.append(VMEM)
    result = pl.pallas_call(
        functools.partial(
            second_kernel, which, blocks, len(groups) if held is None else 0, len(extra)
        ),
        out_shape=out_shape,
        in_specs=[VMEM] * len(fixed) + [ANY] * len(extra),
        out_specs=out_specs,
        scratch_shapes=[
            pltpu.VMEM((mine, width, columns), BF16),
            pltpu.SemaphoreType.DMA((mine,)),
        ],
        input_output_aliases={len(fixed): 0} if extra else {},
        compiler_params=pltpu.CompilerParams(vmem_limit_bytes=16 * MIB),
        cost_estimate=pl.CostEstimate(
            flops=4 * mine * rows * width * columns, bytes_accessed=10 * MIB, transcendentals=0
        ),
        name="second_product",
    )(*fixed, *extra)
    return (result[0], result[1] if held is None else held)


def ring_pairs(distance):
    return [(RING[i], RING[(i + distance) % 4]) for i in range(4)]


def other_core(value):
    return lax.ppermute(value, "rep", SWAP)


def to_x(value):
    return lax.ppermute(value, "vir", SWAP)


def to_y(value):
    return lax.ppermute(value, "grp", SWAP)


def to_z(value, distance=1):
    return lax.ppermute(value, "ao", ring_pairs(distance))


def exchange_small(half_ints, coeff, plan, shift):
    z, x, y = lax.axis_index("ao"), lax.axis_index("vir"), lax.axis_index("grp")
    quarter = y * 2 + x
    gray = lambda n: n ^ (n >> 1)
    owner = [gray((gray(z) + k) & 3) for k in range(4)]
    rows = coeff.shape[0]
    half = rows // 2
    together = lax.optimization_barrier
    join = lambda a, b: jnp.concatenate([a, b], axis=0)

    own = lax.dynamic_slice_in_dim(coeff, quarter * LANES, LANES, 1)
    t = [
        lax.dynamic_index_in_dim(half_ints[:, 0], owner[k], 0, False) for k in range(4)
    ]
    z1, t, group0 = together((to_z(own), t, stay(coeff)))
    x1, y1, z2, t, plan = together((to_x(z1), to_y(z1), to_z(z1), t, plan))
    x2, y2, z3, t1, t = together(
        (to_x(join(z2, y1[:half])), to_y(join(z2, x1[half:])), to_z(z2), to_z(t[1], 1), t)
    )
    group1 = assemble(z1, x1, y1, x2, y2)
    early = shift(plan, 0, [t[0], t1])
    early, last = together((early, t[2]))
    t2, t3 = to_z(last, 2), to_z(t[3], 3)
    x3, y3, group1, early = together(
        (to_x(join(z3, y2[:half])), to_y(join(z3, x2[half:rows])), group1, early)
    )
    group2 = assemble(z2, x2, y2, x3, y3)
    late = shift(plan, 2 * t2.shape[0], [t2, t3])
    x4, y4, late = together((to_x(y3[:half]), to_y(x3[half:rows]), late))
    group3 = assemble(z3, x3, y3, x4, y4)
    return [group0, group1, group2, group3], [early, late], [], plan


def exchange_any(half_ints, coeff):
    count = lax.axis_size("ao")
    gathered = lax.all_gather(coeff, "ao", axis=1, tiled=True)
    width = gathered.shape[1] // GROUPS
    tiles = lax.all_to_all(half_ints, "ao", split_axis=0, concat_axis=2, tiled=True)[0, 0]
    groups = [gathered[:, g * width : (g + 1) * width] for g in range(GROUPS)]
    return gathered, groups, tiles


def local(half_ints, coeff, eps_occ, eps_vir, pair_occ, tile_list, shell_extra):
    sizes = tuple(lax.axis_size(name) for name in ("grp", "ao", "vir"))
    rows, width = coeff.shape
    full_width = width * sizes[1]
    b_width = full_width // sizes[2]
    vir = lax.axis_index("vir")
    ringed = sizes == (2, 4, 2) and width == 4 * LANES
    plan, *energies = make_plan(
        tuple(range(4)) if ringed else (None,), tile_list, shell_extra, pair_occ, eps_occ,
        eps_vir.reshape(1, -1), rows, full_width // lax.axis_size("rep"), b_width,
    )
    if ringed:
        groups, shifted, late, plan = exchange_small(half_ints, coeff, plan, shift_tiles)
        own, blocks = groups, b_width // width
    else:
        gathered, groups, tiles = exchange_any(half_ints, coeff)
        own, blocks = [lax.dynamic_slice_in_dim(gathered, vir * b_width, b_width, 1)], 1
        shifted, late = [shift_tiles(plan, 0, [tiles])], []
    others = [other_core(g) for g in groups]
    other = others if ringed else [other_core(own[0])]
    out = held = None
    for which in range(blocks):
        some = slice(which, GROUPS - 1 + which) if ringed else slice(None)
        middle, shifted = first_product(
            plan, shifted, late, own[some], other[some], which, blocks
        )
        middle, shifted = lax.optimization_barrier((middle, shifted))
        late = []
        both = (middle, other_core(middle))
        out, held = second_product(
            which, blocks, energies, both, [*groups, *others], held, out
        )
    return out


def solution(mesh):
    in_specs = (
        P("grp", "rep", "ao", None, None),
        P("rep", "ao"),
        P(),
        P(),
        P(("grp", "ao"), None),
        P("rep", None, None),
        P(),
    )
    out_specs = P(("grp", "ao"), "rep", "vir")
    return jax.shard_map(local, mesh=mesh, in_specs=in_specs, out_specs=out_specs, check_vma=False)
```

```python
import functools

import jax
import jax.numpy as jnp
from jax import lax
from jax.experimental import pallas as pl
from jax.experimental.pallas import tpu as pltpu
from jax.sharding import PartitionSpec as P

TILE = 128
HALF_BLK = 12
LANES = 128
ROWS_WIN = 144
COLS_WIN = 256
GROUPS = 4
UNROLL = 12
SHIFT_UNROLL = 6
RING = (0, 1, 3, 2)
SWAP = ((0, 1), (1, 0))
F32 = jnp.float32
BF16 = jnp.bfloat16
SMEM = pl.BlockSpec(memory_space=pltpu.SMEM)
VMEM = pl.BlockSpec(memory_space=pltpu.VMEM)
ANY = pl.BlockSpec(memory_space=pl.ANY)
MIB = 1 << 20


def ring_group(step):
    z = lax.axis_index("ao")
    spot = ((z ^ (z >> 1)) - step) & 3
    return spot ^ (spot >> 1)


def plan_kernel(slots, count, rows_half, a_width, listed, extra, pair_occ, eps_occ, eps_vir, plan, by_col, by_row, offsets):
    core = lax.axis_index("rep")

    def lay(k, start):
        start = jnp.where(k == HALF_BLK, 0, start)
        offsets[k] = start
        return start + TILE // 2 + extra[k // HALF_BLK, lax.rem(k, HALF_BLK)]

    lax.fori_loop(0, 2 * HALF_BLK, lay, jnp.int32(0))
    for r, slot in enumerate(slots):
        first = 0 if slot is None else ring_group(slot) * count

        def one(i, carry, r=r, first=first):
            m = listed[0, first + i, 0]
            k = listed[0, first + i, 1]
            half_k = k // HALF_BLK
            off_m = offsets[core * HALF_BLK + m]
            off_k = offsets[k]
            base_m = (off_m // 16) * 16
            base_k = jnp.minimum((off_k // LANES) * LANES, rows_half - COLS_WIN)
            at = r * count + i
            plan[0, at] = base_m
            plan[1, at] = base_k
            plan[2, at] = jnp.where(half_k == core, 0, 1)
            plan[3, at] = off_m - base_m
            plan[4, at] = off_k - base_k
            plan[5, at] = TILE // 2 + extra[core, m]
            plan[6, at] = TILE // 2 + extra[half_k, lax.rem(k, HALF_BLK)]
            return carry

        lax.fori_loop(0, count, one, 0)
    energy = eps_occ[pair_occ[0, 0]] + eps_occ[pair_occ[0, 1]]
    columns = by_col.shape[1]
    start = pl.multiple_of(lax.axis_index("vir") * columns, LANES)
    by_col[...] = energy - eps_vir[:, pl.ds(start, columns)]
    for k in range(a_width // LANES):
        start = pl.multiple_of(core * a_width + k * LANES, LANES)
        row = jnp.broadcast_to(eps_vir[:, pl.ds(start, LANES)], (LANES, LANES))
        by_row[k * LANES : (k + 1) * LANES, :] = jnp.transpose(row)


def make_plan(slots, listed, shell_extra, pair_occ, eps_occ, eps_vir, rows_half, a_width, b_width):
    total = listed.shape[1]
    return pl.pallas_call(
        functools.partial(plan_kernel, slots, total // len(slots), rows_half, a_width),
        out_shape=(
            jax.ShapeDtypeStruct((7, total), jnp.int32),
            jax.ShapeDtypeStruct((1, b_width), F32),
            jax.ShapeDtypeStruct((a_width, LANES), F32),
        ),
        in_specs=[SMEM] * 4 + [VMEM],
        out_specs=(SMEM, VMEM, VMEM),
        scratch_shapes=[pltpu.SMEM((2 * HALF_BLK,), jnp.int32)],
        compiler_params=pltpu.CompilerParams(vmem_limit_bytes=6 * MIB),
        cost_estimate=pl.CostEstimate(flops=0, bytes_accessed=2 * MIB, transcendentals=0),
        name="make_plan",
    )(listed, shell_extra, pair_occ, eps_occ, eps_vir)


def shift_loop(plan, first, held, shifted):
    down_from = lax.broadcasted_iota(jnp.int32, (ROWS_WIN, TILE), 1)
    down = lax.broadcasted_iota(jnp.int32, (ROWS_WIN, TILE), 0) - down_from
    right_from = lax.broadcasted_iota(jnp.int32, (TILE, COLS_WIN), 0)
    right = lax.broadcasted_iota(jnp.int32, (TILE, COLS_WIN), 1) - right_from

    def some(group, carry):
        moved = []
        for u in range(SHIFT_UNROLL):
            i = group * SHIFT_UNROLL + u
            at = first + i
            take_m = jnp.where((down == plan[3, at]) & (down_from < plan[5, at]), 1.0, 0.0)
            take_k = jnp.where((right == plan[4, at]) & (right_from < plan[6, at]), 1.0, 0.0)
            value = jnp.dot(take_m.astype(BF16), held[i], preferred_element_type=F32)
            moved.append((i, value.astype(BF16), take_k.astype(BF16)))
        for i, value, take_k in moved:
            value = jnp.dot(value, take_k, preferred_element_type=F32)
            shifted[i] = value.astype(BF16)
        return carry

    lax.fori_loop(0, held.shape[0] // SHIFT_UNROLL, some, 0)


def tile_copies(tiles, held, sems):
    count = tiles[0].shape[0]
    return [
        pltpu.make_async_copy(ref, held.at[pl.ds(r * count, count)], sems.at[r])
        for r, ref in enumerate(tiles)
    ]


def shift_kernel(first, n_refs, *refs):
    plan = refs[0]
    tiles = refs[1 : 1 + n_refs]
    shifted, held, sems = refs[1 + n_refs :]
    copies = tile_copies(tiles, held, sems)
    for copy in copies:
        copy.start()
    for copy in copies:
        copy.wait()
    shift_loop(plan, first, held, shifted)


def shift_tiles(plan, first, tiles):
    total = sum(t.shape[0] for t in tiles)
    return pl.pallas_call(
        functools.partial(shift_kernel, first, len(tiles)),
        out_shape=jax.ShapeDtypeStruct((total, ROWS_WIN, COLS_WIN), BF16),
        in_specs=[SMEM] + [ANY] * len(tiles),
        out_specs=VMEM,
        scratch_shapes=[
            pltpu.VMEM((total, TILE, TILE), BF16),
            pltpu.SemaphoreType.DMA((len(tiles),)),
        ],
        compiler_params=pltpu.CompilerParams(vmem_limit_bytes=14 * MIB),
        cost_estimate=pl.CostEstimate(flops=0, bytes_accessed=8 * MIB, transcendentals=0),
        name="shift_tiles",
    )(plan, *tiles)


def stay_kernel(value, out):
    out[...] = value[...]


def stay(value):
    return pl.pallas_call(
        stay_kernel,
        out_shape=jax.ShapeDtypeStruct(value.shape, value.dtype),
        in_specs=[VMEM],
        out_specs=VMEM,
        compiler_params=pltpu.CompilerParams(vmem_limit_bytes=8 * MIB),
        cost_estimate=pl.CostEstimate(flops=0, bytes_accessed=3 * MIB, transcendentals=0),
        name="stay",
    )(value)


def assemble_kernel(own, by_x, by_y, far_x, far_y, out, sems):
    rows = own.shape[0]
    half = rows // 2
    q = lax.axis_index("grp") * 2 + lax.axis_index("vir")
    parts = (
        (own, 0, rows, q, 0),
        (by_x, 0, rows, q ^ 1, 0),
        (by_y, 0, rows, q ^ 2, 0),
        (far_x, far_x.shape[0] - half, half, q ^ 3, 0),
        (far_y, far_y.shape[0] - half, half, q ^ 3, half),
    )
    copies = []
    for piece, start, count, at, first in parts:
        lanes = pl.ds(pl.multiple_of(at * LANES, LANES), LANES)
        copies.append(
            pltpu.make_async_copy(
                piece.at[pl.ds(start, count)], out.at[pl.ds(first, count), lanes],
                sems.at[len(copies)],
            )
        )
    for copy in copies:
        copy.start()
    for copy in copies:
        copy.wait()


def assemble(*pieces):
    rows = pieces[0].shape[0]
    return pl.pallas_call(
        assemble_kernel,
        out_shape=jax.ShapeDtypeStruct((rows, 4 * LANES), BF16),
        in_specs=[ANY] * 5,
        out_specs=VMEM,
        scratch_shapes=[pltpu.SemaphoreType.DMA((5,))],
        compiler_params=pltpu.CompilerParams(vmem_limit_bytes=8 * MIB),
        cost_estimate=pl.CostEstimate(flops=0, bytes_accessed=3 * MIB, transcendentals=0),
        name="assemble",
    )(*pieces)


def ring_slot(block):
    z = lax.axis_index("ao")
    return ((z ^ (z >> 1)) - (block ^ (block >> 1))) & 3


def column_block(which, blocks):
    first = lax.axis_index("vir") * blocks
    early, late = ring_slot(first), ring_slot(first + 1)
    swapped = jnp.where(early < late, 0, 1)
    return first + (swapped ^ which)


def pick(slot, first, refs, target):
    for s, ref in enumerate(refs):

        def copy(ref=ref):
            target[...] = ref[...]

        if len(refs) == 1:
            copy()
        else:
            pl.when(slot == first + s)(copy)


def choose_kernel(which, blocks, *refs):
    pick(ring_slot(column_block(which, blocks)), which, refs[:-1], refs[-1])


def choose(which, blocks, groups):
    return pl.pallas_call(
        functools.partial(choose_kernel, which, blocks),
        out_shape=jax.ShapeDtypeStruct(groups[0].shape, BF16),
        in_specs=[VMEM] * len(groups),
        out_specs=VMEM,
        compiler_params=pltpu.CompilerParams(vmem_limit_bytes=8 * MIB),
        cost_estimate=pl.CostEstimate(flops=0, bytes_accessed=MIB, transcendentals=0),
        name="choose",
    )(*groups)


def first_kernel(n_own, n_shifted, n_late, which, blocks, *refs):
    plan = refs[0]
    shifted = list(refs[1 : 1 + n_shifted])
    late = refs[1 + n_shifted : 1 + n_shifted + n_late]
    refs = refs[1 + n_shifted + n_late :]
    own, other = refs[:n_own], refs[n_own : 2 * n_own]
    out = refs[2 * n_own]
    refs = refs[2 * n_own + 1 :]
    if n_late:
        late_shifted, held, total, late_held, sems = refs
        copies = tile_copies(late, late_held, sems)
        for copy in copies:
            copy.start()
    else:
        held, total = refs
    slot = ring_slot(column_block(which, blocks)) if n_own > 1 else 0
    pick(slot, which, own, held.at[0])
    pick(slot, which, other, held.at[1])
    total[...] = jnp.zeros_like(total)
    if n_late:
        for copy in copies:
            copy.wait()
        shift_loop(plan, sum(t.shape[0] for t in shifted), late_held, late_shifted)
        shifted.append(late_shifted)
    before = 0
    for tiles in shifted:

        def add(i, carry, before=before, tiles=tiles):
            sums = []
            for u in range(UNROLL):
                n = i * UNROLL + u
                base_k = pl.multiple_of(plan[1, before + n], LANES)
                window = held[plan[2, before + n], pl.ds(base_k, COLS_WIN), :]
                sums.append((n, jnp.dot(tiles[n], window, preferred_element_type=F32)))
            for n, value in sums:
                base_m = pl.multiple_of(plan[0, before + n], 16)
                total[pl.ds(base_m, ROWS_WIN), :] += value
            return carry

        lax.fori_loop(0, tiles.shape[0] // UNROLL, add, 0)
        before += tiles.shape[0]
    out[...] = total[: out.shape[0], :].astype(BF16)


def first_product(plan, shifted, late, own, other, which, blocks):
    rows, width = own[0].shape
    n_tiles = plan.shape[1]
    n_late = sum(t.shape[0] for t in late)
    out_shape = [jax.ShapeDtypeStruct((rows, width), BF16)]
    scratch = [
        pltpu.VMEM((2, rows, width), BF16),
        pltpu.VMEM((rows + TILE, width), F32),
    ]
    if late:
        out_shape.append(jax.ShapeDtypeStruct((n_late, ROWS_WIN, COLS_WIN), BF16))
        scratch += [
            pltpu.VMEM((n_late, TILE, TILE), BF16),
            pltpu.SemaphoreType.DMA((len(late),)),
        ]
    result = pl.pallas_call(
        functools.partial(first_kernel, len(own), len(shifted), len(late), which, blocks),
        out_shape=out_shape,
        in_specs=[SMEM] + [VMEM] * len(shifted) + [ANY] * len(late) + [VMEM] * (2 * len(own)),
        out_specs=[VMEM] * len(out_shape),
        scratch_shapes=scratch,
        compiler_params=pltpu.CompilerParams(vmem_limit_bytes=14 * MIB),
        cost_estimate=pl.CostEstimate(
            flops=n_tiles * 4 * ROWS_WIN * COLS_WIN * width, bytes_accessed=6 * MIB,
            transcendentals=0,
        ),
        name="first_product",
    )(plan, *shifted, *late, *own, *other)
    return result[0], [*shifted, *result[1:]]


def send_kernel(ringed, middle, *refs):
    groups = refs[:GROUPS]
    out, held = refs[GROUPS:]
    mine = GROUPS // 2
    for i in range(mine):
        wanted = (1 - lax.axis_index("rep")) * mine + i
        pick(ring_slot(wanted) if ringed else wanted, 0, groups, held.at[i])
    dims = (((0,), (0,)), ((), ()))
    for i in range(mine):
        out[i] = lax.dot_general(
            held[i], middle[...], dims, preferred_element_type=F32
        ).astype(BF16)


def send_product(middle, groups, ringed):
    rows, width = groups[0].shape
    columns = middle.shape[1]
    mine = GROUPS // 2
    return pl.pallas_call(
        functools.partial(send_kernel, ringed),
        out_shape=jax.ShapeDtypeStruct((mine, width, columns), BF16),
        in_specs=[VMEM] * (1 + GROUPS),
        out_specs=VMEM,
        scratch_shapes=[pltpu.VMEM((mine, rows, width), BF16)],
        compiler_params=pltpu.CompilerParams(vmem_limit_bytes=12 * MIB),
        cost_estimate=pl.CostEstimate(
            flops=2 * mine * rows * width * columns, bytes_accessed=5 * MIB, transcendentals=0
        ),
        name="send_product",
    )(middle, *groups)


def keep_kernel(which, blocks, n_before, *refs):
    by_col, by_row, middle, got = refs[:4]
    groups = refs[4 : 4 + GROUPS]
    out, held, ready, out_sems = refs[4 + GROUPS + n_before :]
    mine = GROUPS // 2
    width = held.shape[2]
    columns = middle.shape[1]
    for i in range(mine):
        wanted = lax.axis_index("rep") * mine + i
        pick(ring_slot(wanted) if blocks > 1 else wanted, 0, groups, held.at[i])
    if blocks > 1:
        block = column_block(which, blocks) - lax.axis_index("vir") * blocks
        column = pl.multiple_of(block * columns, LANES)
    else:
        column = 0
    dims = (((0,), (0,)), ((), ()))
    stores = []
    for i in range(mine):
        total = lax.dot_general(held[i], middle[...], dims, preferred_element_type=F32)
        total += got[i].astype(F32)
        tall = by_row[i * width : (i + 1) * width, :]
        tall = jnp.concatenate([tall] * (columns // LANES), axis=1)
        ready[i] = (total / (by_col[:, pl.ds(column, columns)] - tall)).astype(BF16)
        store = pltpu.make_async_copy(
            ready.at[i], out.at[0, pl.ds(i * width, width), pl.ds(column, columns)], out_sems.at[i]
        )
        store.start()
        stores.append(store)
    for store in stores:
        store.wait()


def keep_product(which, blocks, energies, middle, got, groups, before):
    rows, width = groups[0].shape
    columns = middle.shape[1]
    mine = GROUPS // 2
    extra = [] if before is None else [before]
    fixed = [*energies, middle, got, *groups]
    return pl.pallas_call(
        functools.partial(keep_kernel, which, blocks, len(extra)),
        out_shape=jax.ShapeDtypeStruct((1, mine * width, blocks * columns), BF16),
        in_specs=[VMEM] * len(fixed) + [ANY] * len(extra),
        out_specs=ANY,
        scratch_shapes=[
            pltpu.VMEM((mine, rows, width), BF16),
            pltpu.VMEM((mine, width, columns), BF16),
            pltpu.SemaphoreType.DMA((mine,)),
        ],
        input_output_aliases={len(fixed): 0} if extra else {},
        compiler_params=pltpu.CompilerParams(vmem_limit_bytes=14 * MIB),
        cost_estimate=pl.CostEstimate(
            flops=2 * mine * rows * width * columns, bytes_accessed=6 * MIB, transcendentals=0
        ),
        name="keep_product",
    )(*fixed, *extra)


def ring_pairs(distance):
    return [(RING[i], RING[(i + distance) % 4]) for i in range(4)]


def other_core(value):
    return lax.ppermute(value, "rep", SWAP)


def to_x(value):
    return lax.ppermute(value, "vir", SWAP)


def to_y(value):
    return lax.ppermute(value, "grp", SWAP)


def to_z(value, distance=1):
    return lax.ppermute(value, "ao", ring_pairs(distance))


def exchange_small(half_ints, coeff, plan, shift):
    z, x, y = lax.axis_index("ao"), lax.axis_index("vir"), lax.axis_index("grp")
    quarter = y * 2 + x
    gray = lambda n: n ^ (n >> 1)
    owner = [gray((gray(z) + k) & 3) for k in range(4)]
    rows = coeff.shape[0]
    half = rows // 2
    together = lax.optimization_barrier
    join = lambda a, b: jnp.concatenate([a, b], axis=0)

    own = lax.dynamic_slice_in_dim(coeff, quarter * LANES, LANES, 1)
    t = [
        lax.dynamic_index_in_dim(half_ints[:, 0], owner[k], 0, False) for k in range(4)
    ]
    z1, t, group0 = together((to_z(own), t, stay(coeff)))
    z2, y1, x1, t, plan = together((to_z(z1), to_y(z1), to_x(z1), t, plan))
    x2, y2, z3, t1, t = together(
        (to_x(join(z2, y1[:half])), to_y(join(z2, x1[half:])), to_z(z2), to_z(t[1], 1), t)
    )
    group1 = assemble(z1, x1, y1, x2, y2)
    early = shift(plan, 0, [t[0], t1])
    t2, t3 = to_z(t[2], 2), to_z(t[3], 3)
    x3, y3, early, group1, t2, t3 = together(
        (to_x(join(z3, y2[:half])), to_y(join(z3, x2[half:rows])), early, group1, t2, t3)
    )
    group2 = assemble(z2, x2, y2, x3, y3)
    blocks = 4 // lax.axis_size("vir")
    first = choose(0, blocks, [group0, group1, group2])
    late = shift(plan, 2 * t2.shape[0], [t2, t3])
    middle, shifted = first_product(
        plan, [early, late], [], [first], [other_core(first)], 0, blocks
    )
    x4, y4, middle = together((to_x(y3[:half]), to_y(x3[half:rows]), middle))
    group3 = assemble(z3, x3, y3, x4, y4)
    return [group0, group1, group2, group3], middle, shifted, plan


def exchange_any(half_ints, coeff):
    count = lax.axis_size("ao")
    gathered = lax.all_gather(coeff, "ao", axis=1, tiled=True)
    width = gathered.shape[1] // GROUPS
    tiles = lax.all_to_all(half_ints, "ao", split_axis=0, concat_axis=2, tiled=True)[0, 0]
    groups = [gathered[:, g * width : (g + 1) * width] for g in range(GROUPS)]
    return gathered, groups, tiles


def local(half_ints, coeff, eps_occ, eps_vir, pair_occ, tile_list, shell_extra):
    sizes = tuple(lax.axis_size(name) for name in ("grp", "ao", "vir"))
    rows, width = coeff.shape
    full_width = width * sizes[1]
    b_width = full_width // sizes[2]
    vir = lax.axis_index("vir")
    ringed = sizes == (2, 4, 2) and width == 4 * LANES
    plan, *energies = make_plan(
        tuple(range(4)) if ringed else (None,), tile_list, shell_extra, pair_occ, eps_occ,
        eps_vir.reshape(1, -1), rows, full_width // lax.axis_size("rep"), b_width,
    )
    if ringed:
        groups, early_middle, shifted, plan = exchange_small(half_ints, coeff, plan, shift_tiles)
        blocks = b_width // width
    else:
        gathered, groups, tiles = exchange_any(half_ints, coeff)
        own, blocks = [lax.dynamic_slice_in_dim(gathered, vir * b_width, b_width, 1)], 1
        shifted = [shift_tiles(plan, 0, [tiles])]
    if ringed:
        own = [choose(1, blocks, groups[1:])]
    other = [other_core(g) for g in own]
    middles, got = [], []
    for which in range(blocks):
        if ringed and which == 0:
            middle = early_middle
        else:
            middle, shifted = first_product(plan, shifted, [], own, other, which, blocks)
        sent = send_product(middle, groups, ringed)
        middle, sent = lax.optimization_barrier((middle, sent))
        middles.append(middle)
        got.append(other_core(sent))
    out = None
    for which in range(blocks):
        out = keep_product(which, blocks, energies, middles[which], got[which], groups, out)
    return out


def solution(mesh):
    in_specs = (
        P("grp", "rep", "ao", None, None),
        P("rep", "ao"),
        P(),
        P(),
        P(("grp", "ao"), None),
        P("rep", None, None),
        P(),
    )
    out_specs = P(("grp", "ao"), "rep", "vir")
    return jax.shard_map(local, mesh=mesh, in_specs=in_specs, out_specs=out_specs, check_vma=False)
```

```python
import functools

import jax
import jax.numpy as jnp
from jax import lax
from jax.experimental import pallas as pl
from jax.experimental.pallas import tpu as pltpu
from jax.sharding import PartitionSpec as P

TILE = 128
HALF_BLK = 12
LANES = 128
ROWS_WIN = 144
COLS_WIN = 256
GROUPS = 4
UNROLL = 12
STORES = 2
SHIFT_UNROLL = 6
RING = (0, 1, 3, 2)
SWAP = ((0, 1), (1, 0))
F32 = jnp.float32
BF16 = jnp.bfloat16
SMEM = pl.BlockSpec(memory_space=pltpu.SMEM)
VMEM = pl.BlockSpec(memory_space=pltpu.VMEM)
ANY = pl.BlockSpec(memory_space=pl.ANY)
MIB = 1 << 20


def ring_group(step):
    z = lax.axis_index("ao")
    spot = ((z ^ (z >> 1)) - step) & 3
    return spot ^ (spot >> 1)


def plan_kernel(slots, count, rows_half, a_width, listed, extra, pair_occ, eps_occ, eps_vir, plan, by_col, by_row, offsets):
    core = lax.axis_index("rep")

    def lay(k, start):
        start = jnp.where(k == HALF_BLK, 0, start)
        offsets[k] = start
        return start + TILE // 2 + extra[k // HALF_BLK, lax.rem(k, HALF_BLK)]

    lax.fori_loop(0, 2 * HALF_BLK, lay, jnp.int32(0))
    for r, slot in enumerate(slots):
        first = 0 if slot is None else ring_group(slot) * count

        def one(i, carry, r=r, first=first):
            m = listed[0, first + i, 0]
            k = listed[0, first + i, 1]
            half_k = k // HALF_BLK
            off_m = offsets[core * HALF_BLK + m]
            off_k = offsets[k]
            base_m = (off_m // 16) * 16
            base_k = jnp.minimum((off_k // LANES) * LANES, rows_half - COLS_WIN)
            at = r * count + i
            plan[0, at] = base_m
            plan[1, at] = base_k
            plan[2, at] = jnp.where(half_k == core, 0, 1)
            plan[3, at] = off_m - base_m
            plan[4, at] = off_k - base_k
            plan[5, at] = TILE // 2 + extra[core, m]
            plan[6, at] = TILE // 2 + extra[half_k, lax.rem(k, HALF_BLK)]
            return carry

        lax.fori_loop(0, count, one, 0)
    energy = eps_occ[pair_occ[0, 0]] + eps_occ[pair_occ[0, 1]]
    columns = by_col.shape[1]
    start = pl.multiple_of(lax.axis_index("vir") * columns, LANES)
    by_col[...] = energy - eps_vir[:, pl.ds(start, columns)]
    for k in range(a_width // LANES):
        start = pl.multiple_of(core * a_width + k * LANES, LANES)
        row = jnp.broadcast_to(eps_vir[:, pl.ds(start, LANES)], (LANES, LANES))
        by_row[k * LANES : (k + 1) * LANES, :] = jnp.transpose(row)


def make_plan(slots, listed, shell_extra, pair_occ, eps_occ, eps_vir, rows_half, a_width, b_width):
    total = listed.shape[1]
    return pl.pallas_call(
        functools.partial(plan_kernel, slots, total // len(slots), rows_half, a_width),
        out_shape=(
            jax.ShapeDtypeStruct((7, total), jnp.int32),
            jax.ShapeDtypeStruct((1, b_width), F32),
            jax.ShapeDtypeStruct((a_width, LANES), F32),
        ),
        in_specs=[SMEM] * 4 + [VMEM],
        out_specs=(SMEM, VMEM, VMEM),
        scratch_shapes=[pltpu.SMEM((2 * HALF_BLK,), jnp.int32)],
        compiler_params=pltpu.CompilerParams(vmem_limit_bytes=6 * MIB),
        cost_estimate=pl.CostEstimate(flops=0, bytes_accessed=2 * MIB, transcendentals=0),
        name="make_plan",
    )(listed, shell_extra, pair_occ, eps_occ, eps_vir)


def shift_loop(plan, first, held, shifted):
    down_from = lax.broadcasted_iota(jnp.int32, (ROWS_WIN, TILE), 1)
    down = lax.broadcasted_iota(jnp.int32, (ROWS_WIN, TILE), 0) - down_from
    right_from = lax.broadcasted_iota(jnp.int32, (TILE, COLS_WIN), 0)
    right = lax.broadcasted_iota(jnp.int32, (TILE, COLS_WIN), 1) - right_from

    def some(group, carry):
        moved = []
        for u in range(SHIFT_UNROLL):
            i = group * SHIFT_UNROLL + u
            at = first + i
            take_m = jnp.where((down == plan[3, at]) & (down_from < plan[5, at]), 1.0, 0.0)
            take_k = jnp.where((right == plan[4, at]) & (right_from < plan[6, at]), 1.0, 0.0)
            value = jnp.dot(take_m.astype(BF16), held[i], preferred_element_type=F32)
            moved.append((i, value.astype(BF16), take_k.astype(BF16)))
        for i, value, take_k in moved:
            value = jnp.dot(value, take_k, preferred_element_type=F32)
            shifted[i] = value.astype(BF16)
        return carry

    lax.fori_loop(0, held.shape[0] // SHIFT_UNROLL, some, 0)


def tile_copies(tiles, held, sems):
    count = tiles[0].shape[0]
    return [
        pltpu.make_async_copy(ref, held.at[pl.ds(r * count, count)], sems.at[r])
        for r, ref in enumerate(tiles)
    ]


def shift_kernel(first, n_refs, *refs):
    plan = refs[0]
    tiles = refs[1 : 1 + n_refs]
    shifted, held, sems = refs[1 + n_refs :]
    copies = tile_copies(tiles, held, sems)
    for copy in copies:
        copy.start()
    for copy in copies:
        copy.wait()
    shift_loop(plan, first, held, shifted)


def shift_tiles(plan, first, tiles):
    total = sum(t.shape[0] for t in tiles)
    return pl.pallas_call(
        functools.partial(shift_kernel, first, len(tiles)),
        out_shape=jax.ShapeDtypeStruct((total, ROWS_WIN, COLS_WIN), BF16),
        in_specs=[SMEM] + [ANY] * len(tiles),
        out_specs=VMEM,
        scratch_shapes=[
            pltpu.VMEM((total, TILE, TILE), BF16),
            pltpu.SemaphoreType.DMA((len(tiles),)),
        ],
        compiler_params=pltpu.CompilerParams(vmem_limit_bytes=14 * MIB),
        cost_estimate=pl.CostEstimate(flops=0, bytes_accessed=8 * MIB, transcendentals=0),
        name="shift_tiles",
    )(plan, *tiles)


def stay_kernel(value, out):
    out[...] = value[...]


def stay(value):
    return pl.pallas_call(
        stay_kernel,
        out_shape=jax.ShapeDtypeStruct(value.shape, value.dtype),
        in_specs=[VMEM],
        out_specs=VMEM,
        compiler_params=pltpu.CompilerParams(vmem_limit_bytes=8 * MIB),
        cost_estimate=pl.CostEstimate(flops=0, bytes_accessed=3 * MIB, transcendentals=0),
        name="stay",
    )(value)


def assemble_kernel(own, by_x, by_y, far_x, far_y, out, sems):
    rows = own.shape[0]
    half = rows // 2
    q = lax.axis_index("grp") * 2 + lax.axis_index("vir")
    parts = (
        (own, 0, rows, q, 0),
        (by_x, 0, rows, q ^ 1, 0),
        (by_y, 0, rows, q ^ 2, 0),
        (far_x, far_x.shape[0] - half, half, q ^ 3, 0),
        (far_y, far_y.shape[0] - half, half, q ^ 3, half),
    )
    copies = []
    for piece, start, count, at, first in parts:
        lanes = pl.ds(pl.multiple_of(at * LANES, LANES), LANES)
        copies.append(
            pltpu.make_async_copy(
                piece.at[pl.ds(start, count)], out.at[pl.ds(first, count), lanes],
                sems.at[len(copies)],
            )
        )
    for copy in copies:
        copy.start()
    for copy in copies:
        copy.wait()


def assemble(*pieces):
    rows = pieces[0].shape[0]
    return pl.pallas_call(
        assemble_kernel,
        out_shape=jax.ShapeDtypeStruct((rows, 4 * LANES), BF16),
        in_specs=[ANY] * 5,
        out_specs=VMEM,
        scratch_shapes=[pltpu.SemaphoreType.DMA((5,))],
        compiler_params=pltpu.CompilerParams(vmem_limit_bytes=8 * MIB),
        cost_estimate=pl.CostEstimate(flops=0, bytes_accessed=3 * MIB, transcendentals=0),
        name="assemble",
    )(*pieces)


def ring_slot(block):
    z = lax.axis_index("ao")
    return ((z ^ (z >> 1)) - (block ^ (block >> 1))) & 3


def column_block(which, blocks):
    first = lax.axis_index("vir") * blocks
    early, late = ring_slot(first), ring_slot(first + 1)
    swapped = jnp.where(early < late, 0, 1)
    return first + (swapped ^ which)


def pick(slot, first, refs, target):
    for s, ref in enumerate(refs):

        def copy(ref=ref):
            target[...] = ref[...]

        if len(refs) == 1:
            copy()
        else:
            pl.when(slot == first + s)(copy)


def choose_kernel(which, blocks, *refs):
    pick(ring_slot(column_block(which, blocks)), which, refs[:-1], refs[-1])


def choose(which, blocks, groups):
    return pl.pallas_call(
        functools.partial(choose_kernel, which, blocks),
        out_shape=jax.ShapeDtypeStruct(groups[0].shape, BF16),
        in_specs=[VMEM] * len(groups),
        out_specs=VMEM,
        compiler_params=pltpu.CompilerParams(vmem_limit_bytes=8 * MIB),
        cost_estimate=pl.CostEstimate(flops=0, bytes_accessed=MIB, transcendentals=0),
        name="choose",
    )(*groups)


def first_kernel(n_own, n_shifted, n_late, which, blocks, *refs):
    plan = refs[0]
    shifted = list(refs[1 : 1 + n_shifted])
    late = refs[1 + n_shifted : 1 + n_shifted + n_late]
    refs = refs[1 + n_shifted + n_late :]
    own, other = refs[:n_own], refs[n_own : 2 * n_own]
    out = refs[2 * n_own]
    refs = refs[2 * n_own + 1 :]
    if n_late:
        late_shifted, held, total, late_held, sems = refs
        copies = tile_copies(late, late_held, sems)
        for copy in copies:
            copy.start()
    else:
        held, total = refs
    slot = ring_slot(column_block(which, blocks)) if n_own > 1 else 0
    pick(slot, which, own, held.at[0])
    pick(slot, which, other, held.at[1])
    total[...] = jnp.zeros_like(total)
    if n_late:
        for copy in copies:
            copy.wait()
        shift_loop(plan, sum(t.shape[0] for t in shifted), late_held, late_shifted)
        shifted.append(late_shifted)
    before = 0
    for tiles in shifted:

        def add(i, carry, before=before, tiles=tiles):
            sums = []
            for u in range(UNROLL):
                n = i * UNROLL + u
                base_k = pl.multiple_of(plan[1, before + n], LANES)
                window = held[plan[2, before + n], pl.ds(base_k, COLS_WIN), :]
                sums.append((n, jnp.dot(tiles[n], window, preferred_element_type=F32)))
            for n, value in sums:
                base_m = pl.multiple_of(plan[0, before + n], 16)
                total[pl.ds(base_m, ROWS_WIN), :] += value
            return carry

        lax.fori_loop(0, tiles.shape[0] // UNROLL, add, 0)
        before += tiles.shape[0]
    out[...] = total[: out.shape[0], :].astype(BF16)


def first_product(plan, shifted, late, own, other, which, blocks):
    rows, width = own[0].shape
    n_tiles = plan.shape[1]
    n_late = sum(t.shape[0] for t in late)
    out_shape = [jax.ShapeDtypeStruct((rows, width), BF16)]
    scratch = [
        pltpu.VMEM((2, rows, width), BF16),
        pltpu.VMEM((rows + TILE, width), F32),
    ]
    if late:
        out_shape.append(jax.ShapeDtypeStruct((n_late, ROWS_WIN, COLS_WIN), BF16))
        scratch += [
            pltpu.VMEM((n_late, TILE, TILE), BF16),
            pltpu.SemaphoreType.DMA((len(late),)),
        ]
    result = pl.pallas_call(
        functools.partial(first_kernel, len(own), len(shifted), len(late), which, blocks),
        out_shape=out_shape,
        in_specs=[SMEM] + [VMEM] * len(shifted) + [ANY] * len(late) + [VMEM] * (2 * len(own)),
        out_specs=[VMEM] * len(out_shape),
        scratch_shapes=scratch,
        compiler_params=pltpu.CompilerParams(vmem_limit_bytes=14 * MIB),
        cost_estimate=pl.CostEstimate(
            flops=n_tiles * 4 * ROWS_WIN * COLS_WIN * width, bytes_accessed=6 * MIB,
            transcendentals=0,
        ),
        name="first_product",
    )(plan, *shifted, *late, *own, *other)
    return result[0], [*shifted, *result[1:]]


def send_body(ringed, middle, groups, out, held):
    mine = GROUPS // 2
    for i in range(mine):
        wanted = (1 - lax.axis_index("rep")) * mine + i
        pick(ring_slot(wanted) if ringed else wanted, 0, groups, held.at[i])
    dims = (((0,), (0,)), ((), ()))
    for i in range(mine):
        out[i] = lax.dot_general(
            held[i], middle[...], dims, preferred_element_type=F32
        ).astype(BF16)


def send_kernel(ringed, middle, *refs):
    send_body(ringed, middle, refs[:GROUPS], *refs[GROUPS:])


def first_and_send_kernel(n_shifted, which, blocks, plan, *refs):
    tiles, refs = refs[:n_shifted], refs[n_shifted:]
    own, other, groups = refs[0], refs[1], refs[2 : 2 + GROUPS]
    out, sent, held, total, left = refs[2 + GROUPS :]
    first_kernel(1, n_shifted, 0, which, blocks, plan, *tiles, own, other, out, held, total)
    send_body(blocks > 1, out, groups, sent, left)


def first_and_send(plan, shifted, own, other, which, blocks, groups):
    rows, width = own.shape
    mine = GROUPS // 2
    left = groups[0].shape[1]
    n_tiles = plan.shape[1]
    return pl.pallas_call(
        functools.partial(first_and_send_kernel, len(shifted), which, blocks),
        out_shape=(
            jax.ShapeDtypeStruct((rows, width), BF16),
            jax.ShapeDtypeStruct((mine, left, width), BF16),
        ),
        in_specs=[SMEM] + [VMEM] * (len(shifted) + 2 + GROUPS),
        out_specs=(VMEM, VMEM),
        scratch_shapes=[
            pltpu.VMEM((2, rows, width), BF16),
            pltpu.VMEM((rows + TILE, width), F32),
            pltpu.VMEM((mine, rows, left), BF16),
        ],
        compiler_params=pltpu.CompilerParams(vmem_limit_bytes=20 * MIB),
        cost_estimate=pl.CostEstimate(
            flops=n_tiles * 4 * ROWS_WIN * COLS_WIN * width + 2 * mine * rows * left * width,
            bytes_accessed=10 * MIB, transcendentals=0,
        ),
        name="first_and_send",
    )(plan, *shifted, own, other, *groups)


def send_product(middle, groups, ringed):
    rows, width = groups[0].shape
    columns = middle.shape[1]
    mine = GROUPS // 2
    return pl.pallas_call(
        functools.partial(send_kernel, ringed),
        out_shape=jax.ShapeDtypeStruct((mine, width, columns), BF16),
        in_specs=[VMEM] * (1 + GROUPS),
        out_specs=VMEM,
        scratch_shapes=[pltpu.VMEM((mine, rows, width), BF16)],
        compiler_params=pltpu.CompilerParams(vmem_limit_bytes=12 * MIB),
        cost_estimate=pl.CostEstimate(
            flops=2 * mine * rows * width * columns, bytes_accessed=5 * MIB, transcendentals=0
        ),
        name="send_product",
    )(middle, *groups)


def keep_kernel(which, blocks, n_groups, n_before, *refs):
    by_col, by_row, middle, got = refs[:4]
    groups = refs[4 : 4 + n_groups]
    mine = GROUPS // 2
    if n_groups == 1:
        held = groups[0]
        out, ready, out_sems = refs[4 + n_groups + n_before :]
    else:
        out, held, ready, out_sems = refs[4 + n_groups + n_before :]
        for i in range(mine):
            wanted = lax.axis_index("rep") * mine + i
            pick(ring_slot(wanted) if blocks > 1 else wanted, 0, groups, held.at[i])
    width = held.shape[2]
    columns = middle.shape[1]
    if blocks > 1:
        block = column_block(which, blocks) - lax.axis_index("vir") * blocks
        column = pl.multiple_of(block * columns, LANES)
    else:
        column = 0
    dims = (((0,), (0,)), ((), ()))
    stores = []
    part = width // STORES
    for i in range(mine):
        for q in range(STORES):
            some = slice(q * part, (q + 1) * part)
            total = lax.dot_general(held[i, :, some], middle[...], dims, preferred_element_type=F32)
            total += got[i, some].astype(F32)
            row = i * width + q * part
            tall = by_row[row : row + part, :]
            tall = jnp.concatenate([tall] * (columns // LANES), axis=1)
            ready[i, some] = (total / (by_col[:, pl.ds(column, columns)] - tall)).astype(BF16)
            store = pltpu.make_async_copy(
                ready.at[i, some], out.at[0, pl.ds(row, part), pl.ds(column, columns)],
                out_sems.at[i * STORES + q],
            )
            store.start()
            stores.append(store)
    for store in stores:
        store.wait()


def keep_product(which, blocks, energies, middle, got, groups, before):
    rows, columns = middle.shape
    mine, width, _ = got.shape
    extra = [] if before is None else [before]
    fixed = [*energies, middle, got, *groups]
    out_shape = [jax.ShapeDtypeStruct((1, mine * width, blocks * columns), BF16)]
    out_specs = [ANY]
    if len(groups) > 1:
        out_shape.append(jax.ShapeDtypeStruct((mine, rows, width), BF16))
        out_specs.append(VMEM)
    result = pl.pallas_call(
        functools.partial(keep_kernel, which, blocks, len(groups), len(extra)),
        out_shape=out_shape,
        in_specs=[VMEM] * len(fixed) + [ANY] * len(extra),
        out_specs=out_specs,
        scratch_shapes=[
            pltpu.VMEM((mine, width, columns), BF16),
            pltpu.SemaphoreType.DMA((mine * STORES,)),
        ],
        input_output_aliases={len(fixed): 0} if extra else {},
        compiler_params=pltpu.CompilerParams(vmem_limit_bytes=14 * MIB),
        cost_estimate=pl.CostEstimate(
            flops=2 * mine * rows * width * columns, bytes_accessed=6 * MIB, transcendentals=0
        ),
        name="keep_product",
    )(*fixed, *extra)
    return result[0], [*result[1:]] or groups


def ring_pairs(distance):
    return [(RING[i], RING[(i + distance) % 4]) for i in range(4)]


def other_core(value):
    return lax.ppermute(value, "rep", SWAP)


def to_x(value):
    return lax.ppermute(value, "vir", SWAP)


def to_y(value):
    return lax.ppermute(value, "grp", SWAP)


def to_z(value, distance=1):
    return lax.ppermute(value, "ao", ring_pairs(distance))


def exchange_small(half_ints, coeff, plan, shift):
    z, x, y = lax.axis_index("ao"), lax.axis_index("vir"), lax.axis_index("grp")
    quarter = y * 2 + x
    gray = lambda n: n ^ (n >> 1)
    owner = [gray((gray(z) + k) & 3) for k in range(4)]
    rows = coeff.shape[0]
    half = rows // 2
    together = lax.optimization_barrier
    join = lambda a, b: jnp.concatenate([a, b], axis=0)

    own = lax.dynamic_slice_in_dim(coeff, quarter * LANES, LANES, 1)
    t = [
        lax.dynamic_index_in_dim(half_ints[:, 0], owner[k], 0, False) for k in range(4)
    ]
    z1, t, group0 = together((to_z(own), t, stay(coeff)))
    z2, y1, x1, t, plan = together((to_z(z1), to_y(z1), to_x(z1), t, plan))
    x2, y2, z3, t1, t = together(
        (to_x(join(z2, y1[:half])), to_y(join(z2, x1[half:])), to_z(z2), to_z(t[1], 1), t)
    )
    group1 = assemble(z1, x1, y1, x2, y2)
    early = shift(plan, 0, [t[0], t1])
    t2, t3 = to_z(t[2], 2), to_z(t[3], 3)
    x3, y3, early, group1, t2, t3 = together(
        (to_x(join(z3, y2[:half])), to_y(join(z3, x2[half:rows])), early, group1, t2, t3)
    )
    group2 = assemble(z2, x2, y2, x3, y3)
    blocks = 4 // lax.axis_size("vir")
    first = choose(0, blocks, [group0, group1, group2])
    late = shift(plan, 2 * t2.shape[0], [t2, t3])
    middle, shifted = first_product(
        plan, [early, late], [], [first], [other_core(first)], 0, blocks
    )
    x4, y4, middle = together((to_x(y3[:half]), to_y(x3[half:rows]), middle))
    group3 = assemble(z3, x3, y3, x4, y4)
    return [group0, group1, group2, group3], middle, shifted, plan


def exchange_any(half_ints, coeff):
    count = lax.axis_size("ao")
    gathered = lax.all_gather(coeff, "ao", axis=1, tiled=True)
    width = gathered.shape[1] // GROUPS
    tiles = lax.all_to_all(half_ints, "ao", split_axis=0, concat_axis=2, tiled=True)[0, 0]
    groups = [gathered[:, g * width : (g + 1) * width] for g in range(GROUPS)]
    return gathered, groups, tiles


def local(half_ints, coeff, eps_occ, eps_vir, pair_occ, tile_list, shell_extra):
    sizes = tuple(lax.axis_size(name) for name in ("grp", "ao", "vir"))
    rows, width = coeff.shape
    full_width = width * sizes[1]
    b_width = full_width // sizes[2]
    vir = lax.axis_index("vir")
    ringed = sizes == (2, 4, 2) and width == 4 * LANES
    plan, *energies = make_plan(
        tuple(range(4)) if ringed else (None,), tile_list, shell_extra, pair_occ, eps_occ,
        eps_vir.reshape(1, -1), rows, full_width // lax.axis_size("rep"), b_width,
    )
    if ringed:
        groups, early_middle, shifted, plan = exchange_small(half_ints, coeff, plan, shift_tiles)
        blocks = b_width // width
    else:
        gathered, groups, tiles = exchange_any(half_ints, coeff)
        own, blocks = [lax.dynamic_slice_in_dim(gathered, vir * b_width, b_width, 1)], 1
        shifted = [shift_tiles(plan, 0, [tiles])]
    if ringed:
        own = [choose(1, blocks, groups[1:])]
    other = [other_core(g) for g in own]
    middles, got = [], []
    for which in range(blocks):
        if ringed and which == 0:
            middle = early_middle
            sent = send_product(middle, groups, ringed)
        else:
            middle, sent = first_and_send(
                plan, shifted, own[0], other[0], which, blocks, groups
            )
        middle, sent = lax.optimization_barrier((middle, sent))
        middles.append(middle)
        got.append(other_core(sent))
    out = None
    for which in range(blocks):
        out, groups = keep_product(
            which, blocks, energies, middles[which], got[which], groups, out
        )
    return out


def solution(mesh):
    in_specs = (
        P("grp", "rep", "ao", None, None),
        P("rep", "ao"),
        P(),
        P(),
        P(("grp", "ao"), None),
        P("rep", None, None),
        P(),
    )
    out_specs = P(("grp", "ao"), "rep", "vir")
    return jax.shard_map(local, mesh=mesh, in_specs=in_specs, out_specs=out_specs, check_vma=False)
```

```python
import functools

import jax
import jax.numpy as jnp
from jax import lax
from jax.experimental import pallas as pl
from jax.experimental.pallas import tpu as pltpu
from jax.sharding import PartitionSpec as P

TILE = 128
HALF_BLK = 12
LANES = 128
ROWS_WIN = 144
COLS_WIN = 256
GROUPS = 4
UNROLL = 12
STORES = 2
SHIFT_UNROLL = 6
RING = (0, 1, 3, 2)
SWAP = ((0, 1), (1, 0))
F32 = jnp.float32
BF16 = jnp.bfloat16
SMEM = pl.BlockSpec(memory_space=pltpu.SMEM)
VMEM = pl.BlockSpec(memory_space=pltpu.VMEM)
ANY = pl.BlockSpec(memory_space=pl.ANY)
MIB = 1 << 20


def ring_group(step):
    z = lax.axis_index("ao")
    spot = ((z ^ (z >> 1)) - step) & 3
    return spot ^ (spot >> 1)


def plan_kernel(slots, count, rows_half, a_width, listed, extra, pair_occ, eps_occ, eps_vir, plan, by_col, by_row, offsets):
    core = lax.axis_index("rep")

    def lay(k, start):
        start = jnp.where(k == HALF_BLK, 0, start)
        offsets[k] = start
        return start + TILE // 2 + extra[k // HALF_BLK, lax.rem(k, HALF_BLK)]

    lax.fori_loop(0, 2 * HALF_BLK, lay, jnp.int32(0))
    for r, slot in enumerate(slots):
        first = 0 if slot is None else ring_group(slot) * count

        def one(i, carry, r=r, first=first):
            m = listed[0, first + i, 0]
            k = listed[0, first + i, 1]
            half_k = k // HALF_BLK
            off_m = offsets[core * HALF_BLK + m]
            off_k = offsets[k]
            base_m = (off_m // 16) * 16
            base_k = jnp.minimum((off_k // LANES) * LANES, rows_half - COLS_WIN)
            at = r * count + i
            plan[0, at] = base_m
            plan[1, at] = base_k
            plan[2, at] = jnp.where(half_k == core, 0, 1)
            plan[3, at] = off_m - base_m
            plan[4, at] = off_k - base_k
            plan[5, at] = TILE // 2 + extra[core, m]
            plan[6, at] = TILE // 2 + extra[half_k, lax.rem(k, HALF_BLK)]
            return carry

        lax.fori_loop(0, count, one, 0)
    energy = eps_occ[pair_occ[0, 0]] + eps_occ[pair_occ[0, 1]]
    columns = by_col.shape[1]
    start = pl.multiple_of(lax.axis_index("vir") * columns, LANES)
    by_col[...] = energy - eps_vir[:, pl.ds(start, columns)]
    for k in range(a_width // LANES):
        start = pl.multiple_of(core * a_width + k * LANES, LANES)
        row = jnp.broadcast_to(eps_vir[:, pl.ds(start, LANES)], (LANES, LANES))
        by_row[k * LANES : (k + 1) * LANES, :] = jnp.transpose(row)


def make_plan(slots, listed, shell_extra, pair_occ, eps_occ, eps_vir, rows_half, a_width, b_width):
    total = listed.shape[1]
    return pl.pallas_call(
        functools.partial(plan_kernel, slots, total // len(slots), rows_half, a_width),
        out_shape=(
            jax.ShapeDtypeStruct((7, total), jnp.int32),
            jax.ShapeDtypeStruct((1, b_width), F32),
            jax.ShapeDtypeStruct((a_width, LANES), F32),
        ),
        in_specs=[SMEM] * 4 + [VMEM],
        out_specs=(SMEM, VMEM, VMEM),
        scratch_shapes=[pltpu.SMEM((2 * HALF_BLK,), jnp.int32)],
        compiler_params=pltpu.CompilerParams(vmem_limit_bytes=6 * MIB),
        cost_estimate=pl.CostEstimate(flops=0, bytes_accessed=2 * MIB, transcendentals=0),
        name="make_plan",
    )(listed, shell_extra, pair_occ, eps_occ, eps_vir)


def shift_loop(plan, first, held, shifted):
    down_from = lax.broadcasted_iota(jnp.int32, (ROWS_WIN, TILE), 1)
    down = lax.broadcasted_iota(jnp.int32, (ROWS_WIN, TILE), 0) - down_from
    right_from = lax.broadcasted_iota(jnp.int32, (TILE, COLS_WIN), 0)
    right = lax.broadcasted_iota(jnp.int32, (TILE, COLS_WIN), 1) - right_from

    def some(group, carry):
        moved = []
        for u in range(SHIFT_UNROLL):
            i = group * SHIFT_UNROLL + u
            at = first + i
            take_m = jnp.where((down == plan[3, at]) & (down_from < plan[5, at]), 1.0, 0.0)
            take_k = jnp.where((right == plan[4, at]) & (right_from < plan[6, at]), 1.0, 0.0)
            value = jnp.dot(take_m.astype(BF16), held[i], preferred_element_type=F32)
            moved.append((i, value.astype(BF16), take_k.astype(BF16)))
        for i, value, take_k in moved:
            value = jnp.dot(value, take_k, preferred_element_type=F32)
            shifted[i] = value.astype(BF16)
        return carry

    lax.fori_loop(0, held.shape[0] // SHIFT_UNROLL, some, 0)


def tile_copies(tiles, held, sems):
    count = tiles[0].shape[0]
    return [
        pltpu.make_async_copy(ref, held.at[pl.ds(r * count, count)], sems.at[r])
        for r, ref in enumerate(tiles)
    ]


def shift_kernel(first, n_refs, *refs):
    plan = refs[0]
    tiles = refs[1 : 1 + n_refs]
    shifted, held, sems = refs[1 + n_refs :]
    copies = tile_copies(tiles, held, sems)
    for copy in copies:
        copy.start()
    for copy in copies:
        copy.wait()
    shift_loop(plan, first, held, shifted)


def shift_tiles(plan, first, tiles):
    total = sum(t.shape[0] for t in tiles)
    return pl.pallas_call(
        functools.partial(shift_kernel, first, len(tiles)),
        out_shape=jax.ShapeDtypeStruct((total, ROWS_WIN, COLS_WIN), BF16),
        in_specs=[SMEM] + [ANY] * len(tiles),
        out_specs=VMEM,
        scratch_shapes=[
            pltpu.VMEM((total, TILE, TILE), BF16),
            pltpu.SemaphoreType.DMA((len(tiles),)),
        ],
        compiler_params=pltpu.CompilerParams(vmem_limit_bytes=14 * MIB),
        cost_estimate=pl.CostEstimate(flops=0, bytes_accessed=8 * MIB, transcendentals=0),
        name="shift_tiles",
    )(plan, *tiles)


def stay_kernel(value, out):
    out[...] = value[...]


def stay(value):
    return pl.pallas_call(
        stay_kernel,
        out_shape=jax.ShapeDtypeStruct(value.shape, value.dtype),
        in_specs=[VMEM],
        out_specs=VMEM,
        compiler_params=pltpu.CompilerParams(vmem_limit_bytes=8 * MIB),
        cost_estimate=pl.CostEstimate(flops=0, bytes_accessed=3 * MIB, transcendentals=0),
        name="stay",
    )(value)


def assemble_kernel(own, by_x, by_y, far_x, far_y, out, sems):
    rows = own.shape[0]
    half = rows // 2
    q = lax.axis_index("grp") * 2 + lax.axis_index("vir")
    parts = (
        (own, 0, rows, q, 0),
        (by_x, 0, rows, q ^ 1, 0),
        (by_y, 0, rows, q ^ 2, 0),
        (far_x, far_x.shape[0] - half, half, q ^ 3, 0),
        (far_y, far_y.shape[0] - half, half, q ^ 3, half),
    )
    copies = []
    for piece, start, count, at, first in parts:
        lanes = pl.ds(pl.multiple_of(at * LANES, LANES), LANES)
        copies.append(
            pltpu.make_async_copy(
                piece.at[pl.ds(start, count)], out.at[pl.ds(first, count), lanes],
                sems.at[len(copies)],
            )
        )
    for copy in copies:
        copy.start()
    for copy in copies:
        copy.wait()


def assemble(*pieces):
    rows = pieces[0].shape[0]
    return pl.pallas_call(
        assemble_kernel,
        out_shape=jax.ShapeDtypeStruct((rows, 4 * LANES), BF16),
        in_specs=[ANY] * 5,
        out_specs=VMEM,
        scratch_shapes=[pltpu.SemaphoreType.DMA((5,))],
        compiler_params=pltpu.CompilerParams(vmem_limit_bytes=8 * MIB),
        cost_estimate=pl.CostEstimate(flops=0, bytes_accessed=3 * MIB, transcendentals=0),
        name="assemble",
    )(*pieces)


def ring_slot(block):
    z = lax.axis_index("ao")
    return ((z ^ (z >> 1)) - (block ^ (block >> 1))) & 3


def column_block(which, blocks):
    first = lax.axis_index("vir") * blocks
    early, late = ring_slot(first), ring_slot(first + 1)
    swapped = jnp.where(early < late, 0, 1)
    return first + (swapped ^ which)


def pick(slot, first, refs, target):
    for s, ref in enumerate(refs):

        def copy(ref=ref):
            target[...] = ref[...]

        if len(refs) == 1:
            copy()
        else:
            pl.when(slot == first + s)(copy)


def choose_kernel(which, blocks, *refs):
    pick(ring_slot(column_block(which, blocks)), which, refs[:-1], refs[-1])


def last_kernel(blocks, *refs):
    pieces, groups, (out, chosen, sems) = refs[:5], refs[5:7], refs[7:]
    assemble_kernel(*pieces, out, sems)
    pick(ring_slot(column_block(1, blocks)), 1, (*groups, out), chosen)


def assemble_last(blocks, pieces, groups):
    shape = jax.ShapeDtypeStruct(groups[0].shape, BF16)
    return pl.pallas_call(
        functools.partial(last_kernel, blocks),
        out_shape=(shape, shape),
        in_specs=[ANY] * 5 + [VMEM] * 2,
        out_specs=(VMEM, VMEM),
        scratch_shapes=[pltpu.SemaphoreType.DMA((5,))],
        compiler_params=pltpu.CompilerParams(vmem_limit_bytes=10 * MIB),
        cost_estimate=pl.CostEstimate(flops=0, bytes_accessed=4 * MIB, transcendentals=0),
        name="assemble_last",
    )(*pieces, *groups)


def choose(which, blocks, groups):
    return pl.pallas_call(
        functools.partial(choose_kernel, which, blocks),
        out_shape=jax.ShapeDtypeStruct(groups[0].shape, BF16),
        in_specs=[VMEM] * len(groups),
        out_specs=VMEM,
        compiler_params=pltpu.CompilerParams(vmem_limit_bytes=8 * MIB),
        cost_estimate=pl.CostEstimate(flops=0, bytes_accessed=MIB, transcendentals=0),
        name="choose",
    )(*groups)


def first_kernel(n_own, n_shifted, n_late, which, blocks, *refs):
    plan = refs[0]
    shifted = list(refs[1 : 1 + n_shifted])
    late = refs[1 + n_shifted : 1 + n_shifted + n_late]
    refs = refs[1 + n_shifted + n_late :]
    own, other = refs[:n_own], refs[n_own : 2 * n_own]
    out = refs[2 * n_own]
    refs = refs[2 * n_own + 1 :]
    if n_late:
        late_shifted, held, total, late_held, sems = refs
        copies = tile_copies(late, late_held, sems)
        for copy in copies:
            copy.start()
    else:
        held, total = refs
    slot = ring_slot(column_block(which, blocks)) if n_own > 1 else 0
    pick(slot, which, own, held.at[0])
    pick(slot, which, other, held.at[1])
    total[...] = jnp.zeros_like(total)
    if n_late:
        for copy in copies:
            copy.wait()
        shift_loop(plan, sum(t.shape[0] for t in shifted), late_held, late_shifted)
        shifted.append(late_shifted)
    before = 0
    for tiles in shifted:

        def add(i, carry, before=before, tiles=tiles):
            sums = []
            for u in range(UNROLL):
                n = i * UNROLL + u
                base_k = pl.multiple_of(plan[1, before + n], LANES)
                window = held[plan[2, before + n], pl.ds(base_k, COLS_WIN), :]
                sums.append((n, jnp.dot(tiles[n], window, preferred_element_type=F32)))
            for n, value in sums:
                base_m = pl.multiple_of(plan[0, before + n], 16)
                total[pl.ds(base_m, ROWS_WIN), :] += value
            return carry

        lax.fori_loop(0, tiles.shape[0] // UNROLL, add, 0)
        before += tiles.shape[0]
    out[...] = total[: out.shape[0], :].astype(BF16)


def first_product(plan, shifted, late, own, other, which, blocks):
    rows, width = own[0].shape
    n_tiles = plan.shape[1]
    n_late = sum(t.shape[0] for t in late)
    out_shape = [jax.ShapeDtypeStruct((rows, width), BF16)]
    scratch = [
        pltpu.VMEM((2, rows, width), BF16),
        pltpu.VMEM((rows + TILE, width), F32),
    ]
    if late:
        out_shape.append(jax.ShapeDtypeStruct((n_late, ROWS_WIN, COLS_WIN), BF16))
        scratch += [
            pltpu.VMEM((n_late, TILE, TILE), BF16),
            pltpu.SemaphoreType.DMA((len(late),)),
        ]
    result = pl.pallas_call(
        functools.partial(first_kernel, len(own), len(shifted), len(late), which, blocks),
        out_shape=out_shape,
        in_specs=[SMEM] + [VMEM] * len(shifted) + [ANY] * len(late) + [VMEM] * (2 * len(own)),
        out_specs=[VMEM] * len(out_shape),
        scratch_shapes=scratch,
        compiler_params=pltpu.CompilerParams(vmem_limit_bytes=14 * MIB),
        cost_estimate=pl.CostEstimate(
            flops=n_tiles * 4 * ROWS_WIN * COLS_WIN * width, bytes_accessed=6 * MIB,
            transcendentals=0,
        ),
        name="first_product",
    )(plan, *shifted, *late, *own, *other)
    return result[0], [*shifted, *result[1:]]


def send_body(ringed, middle, groups, out, held):
    mine = GROUPS // 2
    for i in range(mine):
        wanted = (1 - lax.axis_index("rep")) * mine + i
        pick(ring_slot(wanted) if ringed else wanted, 0, groups, held.at[i])
    dims = (((0,), (0,)), ((), ()))
    for i in range(mine):
        out[i] = lax.dot_general(
            held[i], middle[...], dims, preferred_element_type=F32
        ).astype(BF16)


def send_kernel(ringed, middle, *refs):
    send_body(ringed, middle, refs[:GROUPS], *refs[GROUPS:])


def first_and_send_kernel(n_shifted, which, blocks, plan, *refs):
    tiles, refs = refs[:n_shifted], refs[n_shifted:]
    own, other, groups = refs[0], refs[1], refs[2 : 2 + GROUPS]
    out, sent, held, total, left = refs[2 + GROUPS :]
    first_kernel(1, n_shifted, 0, which, blocks, plan, *tiles, own, other, out, held, total)
    send_body(blocks > 1, out, groups, sent, left)


def first_and_send(plan, shifted, own, other, which, blocks, groups):
    rows, width = own.shape
    mine = GROUPS // 2
    left = groups[0].shape[1]
    n_tiles = plan.shape[1]
    return pl.pallas_call(
        functools.partial(first_and_send_kernel, len(shifted), which, blocks),
        out_shape=(
            jax.ShapeDtypeStruct((rows, width), BF16),
            jax.ShapeDtypeStruct((mine, left, width), BF16),
        ),
        in_specs=[SMEM] + [VMEM] * (len(shifted) + 2 + GROUPS),
        out_specs=(VMEM, VMEM),
        scratch_shapes=[
            pltpu.VMEM((2, rows, width), BF16),
            pltpu.VMEM((rows + TILE, width), F32),
            pltpu.VMEM((mine, rows, left), BF16),
        ],
        compiler_params=pltpu.CompilerParams(vmem_limit_bytes=20 * MIB),
        cost_estimate=pl.CostEstimate(
            flops=n_tiles * 4 * ROWS_WIN * COLS_WIN * width + 2 * mine * rows * left * width,
            bytes_accessed=10 * MIB, transcendentals=0,
        ),
        name="first_and_send",
    )(plan, *shifted, own, other, *groups)


def send_product(middle, groups, ringed):
    rows, width = groups[0].shape
    columns = middle.shape[1]
    mine = GROUPS // 2
    return pl.pallas_call(
        functools.partial(send_kernel, ringed),
        out_shape=jax.ShapeDtypeStruct((mine, width, columns), BF16),
        in_specs=[VMEM] * (1 + GROUPS),
        out_specs=VMEM,
        scratch_shapes=[pltpu.VMEM((mine, rows, width), BF16)],
        compiler_params=pltpu.CompilerParams(vmem_limit_bytes=12 * MIB),
        cost_estimate=pl.CostEstimate(
            flops=2 * mine * rows * width * columns, bytes_accessed=5 * MIB, transcendentals=0
        ),
        name="send_product",
    )(middle, *groups)


def keep_kernel(which, blocks, n_groups, n_before, *refs):
    by_col, by_row, middle, got = refs[:4]
    groups = refs[4 : 4 + n_groups]
    mine = GROUPS // 2
    if n_groups == 1:
        held = groups[0]
        out, ready, out_sems = refs[4 + n_groups + n_before :]
    else:
        out, held, ready, out_sems = refs[4 + n_groups + n_before :]
        for i in range(mine):
            wanted = lax.axis_index("rep") * mine + i
            pick(ring_slot(wanted) if blocks > 1 else wanted, 0, groups, held.at[i])
    width = held.shape[2]
    columns = middle.shape[1]
    if blocks > 1:
        block = column_block(which, blocks) - lax.axis_index("vir") * blocks
        column = pl.multiple_of(block * columns, LANES)
    else:
        column = 0
    dims = (((0,), (0,)), ((), ()))
    stores = []
    part = width // STORES
    for i in range(mine):
        for q in range(STORES):
            some = slice(q * part, (q + 1) * part)
            total = lax.dot_general(held[i, :, some], middle[...], dims, preferred_element_type=F32)
            total += got[i, some].astype(F32)
            row = i * width + q * part
            tall = by_row[row : row + part, :]
            tall = jnp.concatenate([tall] * (columns // LANES), axis=1)
            ready[i, some] = (total / (by_col[:, pl.ds(column, columns)] - tall)).astype(BF16)
            store = pltpu.make_async_copy(
                ready.at[i, some], out.at[0, pl.ds(row, part), pl.ds(column, columns)],
                out_sems.at[i * STORES + q],
            )
            store.start()
            stores.append(store)
    for store in stores:
        store.wait()


def keep_product(which, blocks, energies, middle, got, groups, before):
    rows, columns = middle.shape
    mine, width, _ = got.shape
    extra = [] if before is None else [before]
    fixed = [*energies, middle, got, *groups]
    out_shape = [jax.ShapeDtypeStruct((1, mine * width, blocks * columns), BF16)]
    out_specs = [ANY]
    if len(groups) > 1:
        out_shape.append(jax.ShapeDtypeStruct((mine, rows, width), BF16))
        out_specs.append(VMEM)
    result = pl.pallas_call(
        functools.partial(keep_kernel, which, blocks, len(groups), len(extra)),
        out_shape=out_shape,
        in_specs=[VMEM] * len(fixed) + [ANY] * len(extra),
        out_specs=out_specs,
        scratch_shapes=[
            pltpu.VMEM((mine, width, columns), BF16),
            pltpu.SemaphoreType.DMA((mine * STORES,)),
        ],
        input_output_aliases={len(fixed): 0} if extra else {},
        compiler_params=pltpu.CompilerParams(vmem_limit_bytes=14 * MIB),
        cost_estimate=pl.CostEstimate(
            flops=2 * mine * rows * width * columns, bytes_accessed=6 * MIB, transcendentals=0
        ),
        name="keep_product",
    )(*fixed, *extra)
    return result[0], [*result[1:]] or groups


def ring_pairs(distance):
    return [(RING[i], RING[(i + distance) % 4]) for i in range(4)]


def other_core(value):
    return lax.ppermute(value, "rep", SWAP)


def to_x(value):
    return lax.ppermute(value, "vir", SWAP)


def to_y(value):
    return lax.ppermute(value, "grp", SWAP)


def to_z(value, distance=1):
    return lax.ppermute(value, "ao", ring_pairs(distance))


def exchange_small(half_ints, coeff, plan, shift):
    z, x, y = lax.axis_index("ao"), lax.axis_index("vir"), lax.axis_index("grp")
    quarter = y * 2 + x
    gray = lambda n: n ^ (n >> 1)
    owner = [gray((gray(z) + k) & 3) for k in range(4)]
    rows = coeff.shape[0]
    half = rows // 2
    together = lax.optimization_barrier
    join = lambda a, b: jnp.concatenate([a, b], axis=0)

    own = lax.dynamic_slice_in_dim(coeff, quarter * LANES, LANES, 1)
    t = [
        lax.dynamic_index_in_dim(half_ints[:, 0], owner[k], 0, False) for k in range(4)
    ]
    z1, t, group0 = together((to_z(own), t, stay(coeff)))
    z2, y1, x1, t, plan = together((to_z(z1), to_y(z1), to_x(z1), t, plan))
    x2, y2, z3, t1, t = together(
        (to_x(join(z2, y1[:half])), to_y(join(z2, x1[half:])), to_z(z2), to_z(t[1], 1), t)
    )
    group1 = assemble(z1, x1, y1, x2, y2)
    early = shift(plan, 0, [t[0], t1])
    t2, t3 = to_z(t[2], 2), to_z(t[3], 3)
    x3, y3, early, group1, t2, t3 = together(
        (to_x(join(z3, y2[:half])), to_y(join(z3, x2[half:rows])), early, group1, t2, t3)
    )
    group2 = assemble(z2, x2, y2, x3, y3)
    blocks = 4 // lax.axis_size("vir")
    first = choose(0, blocks, [group0, group1, group2])
    late = shift(plan, 2 * t2.shape[0], [t2, t3])
    middle, shifted = first_product(
        plan, [early, late], [], [first], [other_core(first)], 0, blocks
    )
    x4, y4, middle = together((to_x(y3[:half]), to_y(x3[half:rows]), middle))
    group3, second = assemble_last(blocks, [z3, x3, y3, x4, y4], [group1, group2])
    return [group0, group1, group2, group3], second, middle, shifted, plan


def exchange_any(half_ints, coeff):
    count = lax.axis_size("ao")
    gathered = lax.all_gather(coeff, "ao", axis=1, tiled=True)
    width = gathered.shape[1] // GROUPS
    tiles = lax.all_to_all(half_ints, "ao", split_axis=0, concat_axis=2, tiled=True)[0, 0]
    groups = [gathered[:, g * width : (g + 1) * width] for g in range(GROUPS)]
    return gathered, groups, tiles


def local(half_ints, coeff, eps_occ, eps_vir, pair_occ, tile_list, shell_extra):
    sizes = tuple(lax.axis_size(name) for name in ("grp", "ao", "vir"))
    rows, width = coeff.shape
    full_width = width * sizes[1]
    b_width = full_width // sizes[2]
    vir = lax.axis_index("vir")
    ringed = sizes == (2, 4, 2) and width == 4 * LANES
    plan, *energies = make_plan(
        tuple(range(4)) if ringed else (None,), tile_list, shell_extra, pair_occ, eps_occ,
        eps_vir.reshape(1, -1), rows, full_width // lax.axis_size("rep"), b_width,
    )
    if ringed:
        groups, second, early_middle, shifted, plan = exchange_small(half_ints, coeff, plan, shift_tiles)
        blocks = b_width // width
    else:
        gathered, groups, tiles = exchange_any(half_ints, coeff)
        own, blocks = [lax.dynamic_slice_in_dim(gathered, vir * b_width, b_width, 1)], 1
        shifted = [shift_tiles(plan, 0, [tiles])]
    if ringed:
        own = [second]
    other = [other_core(g) for g in own]
    middles, got = [], []
    for which in range(blocks):
        if ringed and which == 0:
            middle = early_middle
            sent = send_product(middle, groups, ringed)
        else:
            middle, sent = first_and_send(
                plan, shifted, own[0], other[0], which, blocks, groups
            )
        middle, sent = lax.optimization_barrier((middle, sent))
        middles.append(middle)
        got.append(other_core(sent))
    out = None
    for which in range(blocks):
        out, groups = keep_product(
            which, blocks, energies, middles[which], got[which], groups, out
        )
    return out


def solution(mesh):
    in_specs = (
        P("grp", "rep", "ao", None, None),
        P("rep", "ao"),
        P(),
        P(),
        P(("grp", "ao"), None),
        P("rep", None, None),
        P(),
    )
    out_specs = P(("grp", "ao"), "rep", "vir")
    return jax.shard_map(local, mesh=mesh, in_specs=in_specs, out_specs=out_specs, check_vma=False)
```
